128 devices in a mesh: rep: 8 (over x, core), tp: 16 (over y, z).
Axes of the slice: x: 4, y: 4, z: 4, core: 2. Of those that a mesh axis runs over, the one named last changes fastest.
Arguments:
- queries: bfloat16 [4, 512, 8192], P(None, 'rep', 'tp'), may hold values from -128 to 128
- new_kv: bfloat16 [4, 512, 2048], P(None, 'rep'), may hold values from -4 to 4
- kv_cache: bfloat16 [256, 512, 4096], P('rep', None, 'tp'), may hold values from -12 to 12
- lengths: int32 [4, 512], P(None, 'rep'), may hold values from 1 to 512, as said below
- adapter_ids: int32 [4, 512], P(None, 'rep'), may hold values from 0 to 127, as said below
- owner_slot: int32 [128], replicated, may hold values from 0 to 127, as said below
- panels: bfloat16 [128, 8192, 128], P(('rep', 'tp')), may hold values from -0.1875 to 0.1875
- out_weight: bfloat16 [8192, 8192], P('tp'), may hold values from -0.0625 to 0.0625
Outputs:
- mixed: bfloat16 [4, 512, 8192], P(None, 'rep', 'tp')
The draws below stay inside these ranges and needn't reach their ends.
Inputs may be any that keep to these rules, and one draw needn't show every extreme that they name: `lengths`: in each step some request has exactly 512 cached tokens. `adapter_ids`: pool slot s lies on the device of index s // 1 in rep+tp order. In each step, among the 64 requests of one replica (aligned blocks of 64 rows), at most 16 have adapters whose slots lie on any one replica, and exactly 16 on some replica. `owner_slot`: A permutation.
All inputs are finite; a program needn't handle non-finite values.
Results may differ from the reference program's by a relative error of at most 0.0095.
Values may be sent and summed in bfloat16 or wider, within the bound.
A program may use at most 256 MiB of HBM per device.

```python
import math
import jax
import jax.numpy as jnp
from jax import lax

D = 8192
HQ = 64
KVH = 8
HD = 128
RANK = 64
POOL_DEV = 1
STEPS = 4
REQ_REP = 64
MAXLEN = 512
GROUP = 2
HALF = 32
REQ = 512
CAP = 16
ADAPTERS = 128
N_REP = 8
N_TP = 16


def anchor_keys(key):
    return jnp.clip(jax.random.normal(jax.random.fold_in(key, 101), (REQ, KVH, HD), jnp.float32), -3.5, 3.5)


def owner_table(key):
    return jax.random.permutation(jax.random.fold_in(key, 103), ADAPTERS).astype(jnp.int32)


def draw_queries(key, part):
    key = jax.random.fold_in(key, 1)
    drawn = jnp.clip(jax.random.normal(jax.random.fold_in(key, 2), (STEPS, REQ, HQ, HD), jnp.float32), -5.0, 5.0)
    return drawn.reshape(STEPS, REQ, HQ * HD).astype(jnp.bfloat16)


def draw_new_kv(key, part):
    key = jax.random.fold_in(key, 5)
    drawn = jnp.clip(jax.random.normal(key, (STEPS, REQ, KVH, 2, HD), jnp.float32), -4.0, 4.0)
    return drawn.reshape(STEPS, REQ, KVH * 2 * HD).astype(jnp.bfloat16)


def draw_kv_cache(key, part):
    anchors = anchor_keys(key)
    key = jax.random.fold_in(key, 6)
    drawn = jnp.clip(jax.random.normal(key, (N_REP * HALF, MAXLEN, KVH, GROUP, 2, HD), jnp.float32), -4.0, 4.0)
    placed = anchors.reshape(N_REP, GROUP, HALF, KVH, HD).transpose(0, 2, 3, 1, 4).reshape(N_REP * HALF, KVH, GROUP, HD)
    drawn = drawn.at[:, 0, :, :, 0, :].set(placed)
    return drawn.reshape(N_REP * HALF, MAXLEN, N_TP * 2 * HD).astype(jnp.bfloat16)


def draw_lengths(key, part):
    key = jax.random.fold_in(key, 8)
    replica_caps = jax.random.randint(jax.random.fold_in(key, 1), (STEPS, N_REP, 1), MAXLEN // 8, MAXLEN + 1)
    cache_lengths = jax.random.randint(jax.random.fold_in(key, 2), (STEPS, N_REP, REQ_REP), 1, replica_caps + 1)
    cache_lengths = cache_lengths.reshape(STEPS, REQ)
    longest = jax.random.randint(jax.random.fold_in(key, 3), (STEPS,), 0, REQ)
    cache_lengths = cache_lengths.at[jnp.arange(STEPS), longest].set(MAXLEN)
    return cache_lengths.astype(jnp.int32)


def draw_adapter_ids(key, part):
    slot_order = owner_table(key)
    inverse = jnp.argsort(slot_order).astype(jnp.int32)
    key = jax.random.fold_in(key, 9)

    def replica_block(block_key):
        chosen = jax.random.randint(jax.random.fold_in(block_key, 1), (), 0, N_REP)
        shuffled = jax.random.permutation(jax.random.fold_in(block_key, 2), (N_REP - 1) * CAP)
        others = (shuffled[:REQ_REP - CAP] // CAP).astype(jnp.int32)
        others = others + (others >= chosen).astype(jnp.int32)
        targets = jnp.concatenate([jnp.full((CAP,), chosen, jnp.int32), others])
        targets = jax.random.permutation(jax.random.fold_in(block_key, 3), targets)
        within = jax.random.randint(jax.random.fold_in(block_key, 4), (REQ_REP,), 0, N_TP * POOL_DEV)
        return targets * (N_TP * POOL_DEV) + within
    block_keys = jax.random.split(key, STEPS * N_REP)
    slot_indices = jax.vmap(replica_block)(block_keys).reshape(STEPS, REQ)
    return inverse[slot_indices].astype(jnp.int32)


def draw_owner_slot(key, part):
    return owner_table(key)


def levels(rng, extent, pieces, smallest, largest):
    def one(dim, shards_of):
        steps = jax.random.uniform(jax.random.fold_in(jax.random.fold_in(rng, 6), dim), (shards_of,), jnp.float32, smallest / len(pieces), largest / len(pieces))
        return jnp.repeat(jnp.exp(steps), extent[dim] // shards_of).reshape((-1,) + (1,) * (len(extent) - dim - 1))

    gain = one(*pieces[0])
    for cut in pieces[1:]:
        gain = gain * one(*cut)
    return gain


def gaussian(key, shape, width, reach, shards=(), kind=jnp.bfloat16):
    values = width * jax.random.normal(key, shape, jnp.float32)
    if shards:
        values = values * levels(key, shape, shards, -0.22, 0.18)
    return jnp.clip(values, -reach, reach).astype(kind)


def setup_inputs(seed: int = 0) -> dict:
    key_list = jax.random.split(jax.random.key(seed), 9)
    return {
        "queries": draw_queries(jax.random.fold_in(key_list[8], 71), 0),
        "new_kv": draw_new_kv(jax.random.fold_in(key_list[8], 71), 0),
        "kv_cache": draw_kv_cache(jax.random.fold_in(key_list[8], 71), 0),
        "lengths": draw_lengths(jax.random.fold_in(key_list[8], 71), 0),
        "adapter_ids": draw_adapter_ids(jax.random.fold_in(key_list[8], 71), 0),
        "owner_slot": draw_owner_slot(jax.random.fold_in(key_list[8], 71), 0),
        "panels": gaussian(key_list[6], (ADAPTERS, D, 2 * RANK), (16 * RANK) ** -0.5, 0.1875, ((0, 128),)),
        "out_weight": gaussian(key_list[7], (D, D), D ** -0.5, 0.0625, ((0, 16),)),
    }


ADAPTER_SCALING = 2.0
MASKED = -1e+30

def head_attention(operands, lengths_now):
    query_block, keys_head, values_head, fresh_key, fresh_value = operands
    scale_factor = 1.0 / math.sqrt(HD)
    position_ids = jnp.arange(keys_head.shape[1], dtype=jnp.int32)
    valid_mask = (position_ids[None, :] < lengths_now[:, None])[:, None, :]
    scores = jnp.einsum('rqd,rpd->rqp', query_block, keys_head.astype(jnp.float32)) * scale_factor
    scores = jnp.where(valid_mask, scores, MASKED)
    own_score = jnp.einsum('rqd,rd->rq', query_block, fresh_key.astype(jnp.float32)) * scale_factor
    top_score = jnp.maximum(lax.optimization_barrier(jnp.max(scores, axis=-1)), own_score)
    weights = jnp.where(valid_mask, jnp.exp(scores - top_score[..., None]), 0.0)
    own_weight = jnp.exp(own_score - top_score)
    denominator = lax.optimization_barrier(jnp.sum(weights, axis=-1)) + own_weight
    rounded = lax.optimization_barrier(weights.astype(jnp.bfloat16)).astype(jnp.float32)
    own_rounded = lax.optimization_barrier(own_weight.astype(jnp.bfloat16)).astype(jnp.float32)
    mixed_values = jnp.einsum('rqp,rpd->rqd', rounded, values_head.astype(jnp.float32))
    mixed_values = mixed_values + own_rounded[..., None] * fresh_value.astype(jnp.float32)[:, None, :]
    return (mixed_values / denominator[..., None]).astype(jnp.bfloat16)

def reference(queries, new_kv, kv_cache, lengths, adapter_ids, owner_slot, panels, out_weight):
    group_heads = HQ // KVH
    cache_heads = kv_cache.reshape(N_REP, HALF, MAXLEN, KVH, GROUP, 2, HD)
    cache_heads = cache_heads.transpose(3, 0, 4, 1, 2, 5, 6).reshape(KVH, REQ, MAXLEN, 2, HD)
    keys_all = cache_heads[:, :, :, 0, :]
    values_all = cache_heads[:, :, :, 1, :]

    def adapter_update(operands):
        one_row, one_slot = operands
        one_panel = panels[one_slot]
        shrink_project = jnp.dot(one_row, one_panel[:, :RANK], preferred_element_type=jnp.float32).astype(jnp.bfloat16)
        return jnp.dot(one_panel[:, RANK:], shrink_project, preferred_element_type=jnp.float32)
    result_list = []
    for step_index in range(STEPS):
        query_heads = queries[step_index].astype(jnp.float32).reshape(REQ, KVH, group_heads, HD).transpose(1, 0, 2, 3)
        fresh_kv = new_kv[step_index].reshape(REQ, KVH, 2, HD).transpose(1, 0, 2, 3)
        lengths_now = lengths[step_index]
        attended = lax.map(lambda operands: head_attention(operands, lengths_now), (query_heads, keys_all, values_all, fresh_kv[:, :, 0, :], fresh_kv[:, :, 1, :]))
        decode_attention = attended.transpose(1, 0, 2, 3).reshape(REQ, HQ * HD)
        base_output = jnp.dot(decode_attention, out_weight, preferred_element_type=jnp.float32)
        slot_indices = owner_slot[adapter_ids[step_index]].astype(jnp.int32)
        lowrank_update = lax.map(adapter_update, (decode_attention, slot_indices))
        result_list.append((base_output + ADAPTER_SCALING * lowrank_update).astype(jnp.bfloat16))
    return jnp.stack(result_list, 0)
```

```python
import functools
import math

import jax
import jax.numpy as jnp
from jax import lax
from jax.experimental import pallas as pl
from jax.experimental.pallas import tpu as pltpu
from jax.sharding import PartitionSpec as P

MESH = pl.DeviceIdType.MESH
F32 = jnp.float32
BF16 = jnp.bfloat16

HD = 128
RANK = 64
CAP = 16
LANES = 128
KV_CHUNK = 4
ADAPTER_SCALING = 2.0
MASKED = -1e30


def nt_dot(a, b):
    return lax.dot_general(a, b, (((1,), (1,)), ((), ())), preferred_element_type=F32)


def tn_dot(a, b):
    return lax.dot_general(a, b, (((0,), (0,)), ((), ())), preferred_element_type=F32)


def dot(a, b):
    return jnp.dot(a, b, preferred_element_type=F32)


def iota(shape, dim):
    return lax.broadcasted_iota(jnp.int32, shape, dim)


def kernel(
    n_rep, n_tp, side,
    queries, new_kv, kv_cache, lengths, ids, owners, panels, weight,
    out,
    q_own, q_in, q_rows, o_rows, fresh, cache, w_buf, pan, spread, attn, attn_back, tags, place,
    send_y, recv_y, own_y, send_z, recv_z, own_z, fwd_a, got_a, fwd_b, got_b, base,
    disp, work, part, part_in, shrink, delta, delta_in,
    cache_sem, load_sem, q_sem, pan_send, pan_recv, back_sem,
    y_send, y_recv, z_send, z_recv, a_send, a_recv, b_send, b_recv,
    disp_send, disp_recv, part_send, part_recv, shr_send, shr_recv, del_send, del_recv,
):
    steps, rows, width = out.shape
    half = rows // 2
    heads = width // HD
    per_request = 2 * heads * steps
    total_rows = steps * rows
    part_width = width // 2
    bits = n_tp.bit_length() - 1
    cap_bits = CAP.bit_length() - 1

    rep = lax.axis_index("rep")
    t = lax.axis_index("tp")
    y, z = lax.div(t, side), lax.rem(t, side)
    member, group = lax.rem(t, 2), lax.div(t, 2)
    partner = t + 1 - 2 * member
    mine = pl.multiple_of(member * half, half)
    other = pl.multiple_of((1 - member) * half, half)

    def tp_peer(k):
        dy, dz = lax.div(k, side), lax.rem(k, side)
        return lax.rem(y + dy, side) * side + lax.rem(z + dz, side)

    def rep_peer(k):
        return lax.rem(rep + k, n_rep)

    def remote(src, dst, send, recv, device):
        return pltpu.make_async_remote_copy(
            src_ref=src, dst_ref=dst, send_sem=send, recv_sem=recv, device_id=device, device_id_type=MESH
        )

    def over(low, high, body):
        def run(k, carry):
            body(k)
            return carry

        lax.fori_loop(low, high, run, 0)

    load_q = pltpu.make_async_copy(queries.at[:, pl.ds(mine, half), :], q_own, load_sem.at[0])
    load_fresh = pltpu.make_async_copy(
        new_kv.at[:, pl.ds(mine, half), pl.ds(pl.multiple_of(group * 2 * HD, 2 * HD), 2 * HD)], fresh, load_sem.at[1]
    )
    load_w = pltpu.make_async_copy(weight, w_buf, load_sem.at[2])

    def load_cache(c):
        span = pl.ds(c * KV_CHUNK, KV_CHUNK)
        return pltpu.make_async_copy(kv_cache.at[span], cache.at[span], cache_sem.at[c])

    load_q.start()
    load_fresh.start()
    over(0, half // KV_CHUNK, lambda c: load_cache(c).start())
    load_w.start()

    barrier = pltpu.get_barrier_semaphore()
    over(1, n_tp, lambda k: pl.semaphore_signal(barrier, inc=1, device_id=(rep, tp_peer(k)), device_id_type=MESH))
    over(1, n_rep, lambda k: pl.semaphore_signal(barrier, inc=1, device_id=(rep_peer(k), t), device_id_type=MESH))
    pl.semaphore_wait(barrier, n_tp + n_rep - 2)

    swap_q = remote(queries.at[:, pl.ds(other, half), :], q_in, q_sem.at[0], q_sem.at[1], (rep, partner))
    swap_q.start()
    pan_cols = pl.ds(pl.multiple_of(t * LANES, LANES), LANES)

    def send_pan(k):
        peer = tp_peer(k)
        src = panels.at[0, pl.ds(pl.multiple_of(peer * width, width), width), :]
        return remote(src, pan.at[:, pan_cols], pan_send.at[k], pan_recv.at[k], (rep, peer))

    over(1, n_tp, lambda k: send_pan(k).start())
    keep_pan = pltpu.make_async_copy(
        panels.at[0, pl.ds(pl.multiple_of(t * width, width), width), :], pan.at[:, pan_cols], load_sem.at[3]
    )
    keep_pan.start()

    n_dest = n_rep * CAP
    n_adapters = owners.shape[1]
    diagonal = iota((rows, rows), 0) == iota((rows, rows), 1)
    earlier = jnp.where(iota((rows, rows), 1) < iota((rows, rows), 0), 1.0, 0.0).astype(BF16)
    dest = iota((rows, n_dest), 1)
    for s in range(steps):
        id_row = jnp.broadcast_to(ids[s : s + 1, :].astype(F32), (rows, rows))
        id_col = jnp.sum(jnp.where(diagonal, id_row, 0.0), axis=1, keepdims=True)
        found = iota((rows, n_adapters), 1).astype(F32) == id_col
        owner_row = jnp.broadcast_to(owners[...].astype(F32), (rows, n_adapters))
        slot = jnp.sum(jnp.where(found, owner_row, 0.0), axis=1, keepdims=True).astype(jnp.int32)
        holder = lax.shift_right_logical(slot, bits)
        goes = lax.shift_right_logical(dest, cap_bits) == holder
        rank = dot(earlier, jnp.where(goes, 1.0, 0.0).astype(BF16))
        here = goes & (rank == (dest & (CAP - 1)).astype(F32))
        place[s] = jnp.where(here, 1.0, 0.0).astype(BF16)
        tags[s] = jnp.where(iota((rows, LANES), 1) == (slot & (n_tp - 1)), 1.0, 0.0).astype(BF16)
    spread[...] = jnp.where(
        iota(spread.shape, 0) == lax.shift_right_logical(iota(spread.shape, 1), 7), 1.0, 0.0
    ).astype(BF16)

    load_q.wait()
    load_fresh.wait()
    swap_q.wait()
    for s in range(steps):
        for h in range(heads):
            cols = slice(h * HD, (h + 1) * HD)
            q_rows[pl.ds(h * steps + s, half, stride=per_request), :] = q_own[s, :, cols].astype(F32)
            q_rows[pl.ds((heads + h) * steps + s, half, stride=per_request), :] = q_in[s, :, cols].astype(F32)

    scale = 1.0 / math.sqrt(HD)
    positions = cache.shape[1]

    def attend(i):
        q = q_rows[pl.ds(pl.multiple_of(i * per_request, per_request), per_request), :].astype(BF16)
        step_of = iota((per_request, 1), 0) & (steps - 1)
        limit = jnp.zeros((per_request, 1), jnp.int32)
        for s in range(steps):
            limit = jnp.where(step_of == s, lengths[s, mine + i], limit)
        fresh_rows = fresh[...].reshape(steps * half, 2 * HD)
        scores = nt_dot(q, cache[i, :, :HD]) * scale
        scores = jnp.where(iota(scores.shape, 1) < limit, scores, MASKED)
        own = nt_dot(q, fresh_rows[:, :HD]) * scale
        own = jnp.where(iota(own.shape, 1) == step_of * half + i, own, MASKED)
        top = jnp.maximum(jnp.max(scores, axis=1, keepdims=True), jnp.max(own, axis=1, keepdims=True))
        scores = jnp.exp(scores - top)
        own = jnp.exp(own - top)
        total = jnp.sum(scores, axis=1, keepdims=True) + jnp.sum(own, axis=1, keepdims=True)
        mixed = dot(scores.astype(BF16), cache[i, :, HD:]) + dot(own.astype(BF16), fresh_rows[:, HD:])
        o_rows[pl.ds(pl.multiple_of(i * per_request, per_request), per_request), :] = mixed / total

    def attend_chunk(c):
        load_cache(c).wait()
        for j in range(KV_CHUNK):
            attend(c * KV_CHUNK + j)

    over(0, half // KV_CHUNK, attend_chunk)

    for s in range(steps):
        for h in range(heads):
            cols = slice(h * HD, (h + 1) * HD)
            own_heads = o_rows[pl.ds(h * steps + s, half, stride=per_request), :]
            attn[s, pl.ds(mine, half), cols] = own_heads.astype(BF16)
            far_heads = o_rows[pl.ds((heads + h) * steps + s, half, stride=per_request), :]
            attn_back[s, :, cols] = far_heads.astype(BF16)
    swap_back = remote(
        attn_back, attn.at[:, pl.ds(mine, half), :], back_sem.at[0], back_sem.at[1], (rep, partner)
    )
    swap_back.start()
    swap_back.wait()

    for s in range(steps):
        span = slice(s * CAP, (s + 1) * CAP)
        routed = tn_dot(place[s], attn[s]).astype(BF16)
        disp[:, span, :width] = routed.reshape(n_rep, CAP, width)
        disp[:, span, width:] = tn_dot(place[s], tags[s]).astype(BF16).reshape(n_rep, CAP, LANES)

    def send_disp(k):
        peer = rep_peer(k)
        return remote(disp.at[peer], work.at[rep], disp_send.at[k], disp_recv.at[k], (peer, t))

    over(1, n_rep, lambda k: send_disp(k).start())
    work[rep] = disp[rep]

    load_w.wait()

    def project(block, part):
        cols = pl.ds(pl.multiple_of(block * width + part * part_width, part_width), part_width)
        return dot(attn[...].reshape(total_rows, width), w_buf[:, cols])

    def along_y(d, j):
        device = (rep, lax.rem(y + d, side) * side + z)
        return remote(send_y.at[d - 1, j], recv_y.at[d - 1, j], y_send.at[d - 1, j], y_recv.at[d - 1, j], device)

    def along_z(d, j):
        device = (rep, y * side + lax.rem(z + d, side))
        return remote(send_z.at[d - 1, j], recv_z.at[d - 1, j], z_send.at[d - 1, j], z_recv.at[d - 1, j], device)

    def first_stage(j):
        to_z = lax.rem(z + 1 + j, side)
        to_y = lax.rem(y + 1 + j, side)
        for d in range(1, side):
            send_y[d - 1, j] = project(lax.rem(y + d, side) * side + to_z, 0).astype(BF16)
            along_y(d, j).start()
            send_z[d - 1, j] = project(to_y * side + lax.rem(z + d, side), 1).astype(BF16)
            along_z(d, j).start()
        own_y[j] = project(y * side + to_z, 0)
        own_z[j] = project(to_y * side + z, 1)

    over(0, side, first_stage)

    keep_pan.wait()
    over(1, n_tp, lambda k: send_pan(k).wait_recv())
    over(1, n_rep, lambda k: send_disp(k).wait_recv())
    work_rows = n_rep * steps * CAP
    packed_rows = work_rows // 2
    tile = min(128, packed_rows)
    tile_reps = tile // (steps * CAP)
    low_lanes = iota((tile, LANES), 1) < RANK

    def masks(tags_rows):
        return dot(tags_rows, spread[...])

    def shrink_tile(c):
        x = work[pl.ds(c * tile_reps, tile_reps)].reshape(tile, width + LANES)
        products = dot(x[:, :width], pan[...]) * masks(x[:, width:])
        total = products[:, :LANES]
        for a in range(1, n_tp):
            total = total + products[:, a * LANES : (a + 1) * LANES]
        return total

    n_tiles = packed_rows // tile

    def shrink_pair(c):
        first = shrink_tile(c)
        second = pltpu.roll(shrink_tile(n_tiles + c), RANK, 1)
        part[pl.ds(pl.multiple_of(c * tile, tile), tile), :] = jnp.where(low_lanes, first, second)

    over(0, n_tiles, shrink_pair)

    slab = packed_rows // n_tp

    def slab_of(device):
        return pl.ds(pl.multiple_of(device * slab, slab), slab)

    def send_part(k):
        peer = tp_peer(k)
        return remote(part.at[slab_of(peer)], part_in.at[k], part_send.at[k], part_recv.at[k], (rep, peer))

    over(1, n_tp, lambda k: send_part(k).start())

    def forward_y(j):
        device = (rep, y * side + lax.rem(z + 1 + j, side))
        return remote(fwd_a.at[j], got_a.at[j], a_send.at[j], a_recv.at[j], device)

    def forward_z(j):
        device = (rep, lax.rem(y + 1 + j, side) * side + z)
        return remote(fwd_b.at[j], got_b.at[j], b_send.at[j], b_recv.at[j], device)

    def gathered(own, recv, copy, j):
        total = own[j]
        for d in range(1, side):
            copy(d, j).wait_recv()
            total = total + recv[d - 1, j].astype(F32)
        return total

    def second_stage(j):
        fwd_a[j] = gathered(own_y, recv_y, along_y, j).astype(BF16)
        forward_y(j).start()
        fwd_b[j] = gathered(own_z, recv_z, along_z, j).astype(BF16)
        forward_z(j).start()

    second_stage(0)

    over(1, n_tp, lambda k: send_part(k).wait_recv())
    total = part[slab_of(t), :]
    for k in range(1, n_tp):
        total = total + part_in[k]
    shrink[slab_of(t), :] = total.astype(BF16)

    def send_shrink(k):
        peer = tp_peer(k)
        return remote(shrink.at[slab_of(t)], shrink.at[slab_of(t)], shr_send.at[k], shr_recv.at[k], (rep, peer))

    over(1, n_tp, lambda k: send_shrink(k).start())
    over(1, side - 1, second_stage)

    over(1, n_tp, lambda k: send_shrink(k).wait_recv())

    def expand_tile(c, low):
        shrunk = shrink[pl.ds(pl.multiple_of(c * tile, tile), tile), :].astype(F32)
        if low:
            shrunk = pltpu.roll(shrunk, RANK, 1)
        shrunk = jnp.where(low_lanes, 0.0, shrunk)
        at = c if low else n_tiles + c
        tag = work[pl.ds(at * tile_reps, tile_reps), :, width:].reshape(tile, LANES)
        picked = (masks(tag) * jnp.concatenate([shrunk] * n_tp, axis=1)).astype(BF16)
        result = nt_dot(picked, pan[...]).astype(BF16)
        delta[pl.ds(at * tile_reps, tile_reps)] = result.reshape(tile_reps, steps * CAP, width)

    def expand_pair(c):
        expand_tile(c, True)
        expand_tile(c, False)

    over(0, n_tiles, expand_pair)

    def send_delta(k):
        peer = rep_peer(k)
        return remote(delta.at[peer], delta_in.at[rep], del_send.at[k], del_recv.at[k], (peer, t))

    over(1, n_rep, lambda k: send_delta(k).start())
    delta_in[rep] = delta[rep]

    last = side - 1
    base[:, :part_width] = gathered(own_y, recv_y, along_y, last)
    base[:, part_width:] = gathered(own_z, recv_z, along_z, last)
    for j in range(last):
        forward_y(j).wait_recv()
        base[:, :part_width] += got_a[j].astype(F32)
        forward_z(j).wait_recv()
        base[:, part_width:] += got_b[j].astype(F32)

    over(1, n_rep, lambda k: send_delta(k).wait_recv())
    for s in range(steps):
        rows_in = delta_in[:, s * CAP : (s + 1) * CAP, :].reshape(n_dest, width)
        update = dot(place[s], rows_in)
        out[s] = (base[s * rows : (s + 1) * rows, :] + ADAPTER_SCALING * update).astype(BF16)

    def drain_tp(k):
        send_pan(k).wait_send()
        send_part(k).wait_send()
        send_shrink(k).wait_send()

    def drain_rep(k):
        send_disp(k).wait_send()
        send_delta(k).wait_send()

    def drain_sums(j):
        for d in range(1, side):
            along_y(d, j).wait_send()
            along_z(d, j).wait_send()

    def drain_forward(j):
        forward_y(j).wait_send()
        forward_z(j).wait_send()

    over(1, n_tp, drain_tp)
    over(1, n_rep, drain_rep)
    over(0, side, drain_sums)
    over(0, side - 1, drain_forward)


def shards(n_rep, n_tp, queries, new_kv, kv_cache, lengths, adapter_ids, owner_slot, panels, out_weight):
    side = math.isqrt(n_tp)
    steps, rows, width = queries.shape
    half = rows // 2
    heads = width // HD
    total = steps * rows
    part = width // 2
    per_request = 2 * heads * steps
    work_rows = n_rep * steps * CAP
    dma = pltpu.SemaphoreType.DMA
    vmem = pltpu.VMEM
    hop = side - 1
    scratch = [
        vmem((steps, half, width), BF16),
        vmem((steps, half, width), BF16),
        vmem((half * per_request, HD), F32),
        vmem((half * per_request, HD), F32),
        vmem((steps, half, 2 * HD), BF16),
        vmem(kv_cache.shape, BF16),
        vmem(out_weight.shape, BF16),
        vmem((width, n_tp * LANES), BF16),
        vmem((LANES, n_tp * LANES), BF16),
        vmem((steps, rows, width), BF16),
        vmem((steps, half, width), BF16),
        vmem((steps, rows, LANES), BF16),
        vmem((steps, rows, n_rep * CAP), BF16),
        vmem((hop, side, total, part), BF16),
        vmem((hop, side, total, part), BF16),
        vmem((side, total, part), F32),
        vmem((hop, side, total, part), BF16),
        vmem((hop, side, total, part), BF16),
        vmem((side, total, part), F32),
        vmem((hop, total, part), BF16),
        vmem((hop, total, part), BF16),
        vmem((hop, total, part), BF16),
        vmem((hop, total, part), BF16),
        vmem((total, width), F32),
        vmem((n_rep, steps * CAP, width + LANES), BF16),
        vmem((n_rep, steps * CAP, width + LANES), BF16),
        vmem((work_rows // 2, LANES), F32),
        vmem((n_tp, work_rows // 2 // n_tp, LANES), F32),
        vmem((work_rows // 2, LANES), BF16),
        vmem((n_rep, steps * CAP, width), BF16),
        vmem((n_rep, steps * CAP, width), BF16),
        dma((half // KV_CHUNK,)),
        dma((4,)),
        dma((2,)),
        dma((n_tp,)), dma((n_tp,)),
        dma((2,)),
        dma((hop, side)), dma((hop, side)),
        dma((hop, side)), dma((hop, side)),
        dma((hop,)), dma((hop,)),
        dma((hop,)), dma((hop,)),
        dma((n_rep,)), dma((n_rep,)),
        dma((n_tp,)), dma((n_tp,)),
        dma((n_tp,)), dma((n_tp,)),
        dma((n_rep,)), dma((n_rep,)),
    ]
    hbm = pl.BlockSpec(memory_space=pl.ANY)
    in_vmem = pl.BlockSpec(memory_space=pltpu.VMEM)
    in_smem = pl.BlockSpec(memory_space=pltpu.SMEM)
    return pl.pallas_call(
        functools.partial(kernel, n_rep, n_tp, side),
        out_shape=jax.ShapeDtypeStruct(queries.shape, BF16),
        in_specs=[hbm, hbm, hbm, in_smem, in_vmem, in_vmem, hbm, hbm],
        out_specs=in_vmem,
        scratch_shapes=scratch,
        compiler_params=pltpu.CompilerParams(
            collective_id=0, has_side_effects=True, vmem_limit_bytes=56 * 1024 * 1024
        ),
        cost_estimate=pl.CostEstimate(
            flops=5_000_000_000, bytes_accessed=20_000_000, transcendentals=600_000
        ),
    )(queries, new_kv, kv_cache, lengths, adapter_ids, owner_slot.reshape(1, -1), panels, out_weight)


def solution(mesh):
    placed = (
        P(None, "rep", "tp"),
        P(None, "rep", None),
        P("rep", None, "tp"),
        P(None, "rep"),
        P(None, "rep"),
        P(),
        P(("rep", "tp"), None, None),
        P("tp", None),
    )
    return jax.shard_map(
        functools.partial(shards, mesh.shape["rep"], mesh.shape["tp"]),
        mesh=mesh, in_specs=placed, out_specs=P(None, "rep", "tp"), check_vma=False,
    )
```

```python
import functools
import math

import jax
import jax.numpy as jnp
from jax import lax
from jax.experimental import pallas as pl
from jax.experimental.pallas import tpu as pltpu
from jax.sharding import PartitionSpec as P

MESH = pl.DeviceIdType.MESH
F32 = jnp.float32
BF16 = jnp.bfloat16

HD = 128
RANK = 64
CAP = 16
LANES = 128
KV_CHUNK = 4
ADAPTER_SCALING = 2.0
MASKED = -1e30


def nt_dot(a, b):
    return lax.dot_general(a, b, (((1,), (1,)), ((), ())), preferred_element_type=F32)


def tn_dot(a, b):
    return lax.dot_general(a, b, (((0,), (0,)), ((), ())), preferred_element_type=F32)


def dot(a, b):
    return jnp.dot(a, b, preferred_element_type=F32)


def iota(shape, dim):
    return lax.broadcasted_iota(jnp.int32, shape, dim)


def panel_batches(side):
    def far(v):
        return min(v, side - v)

    offsets = [(dy, dz) for dy in range(side) for dz in range(side) if dy or dz]
    batches = [[], [], []]
    for dy, dz in offsets:
        if far(dy) == far(dz):
            batches[0].append((far(dy), dy, dz))
        elif far(dy) + far(dz) == 2:
            batches[1].append((0, dy, dz))
        else:
            batches[2].append((-far(dy) - far(dz), dy, dz))
    return [[dy * side + dz for _, dy, dz in sorted(batch)] for batch in batches]


def kernel(
    n_rep, n_tp, side,
    queries, new_kv, kv_cache, lengths, ids, owners, panels, weight,
    out,
    q_own, q_in, q_rows, o_rows, fresh, cache, w_buf, pool, pack_a, pack_b, pan_a, pan_b, spread, attn, attn_back, tags, place,
    far_y, hop_y, near_y, in_y, own_y, far_z, hop_z, near_z, in_z, own_z, fwd_a, got_a, fwd_b, got_b, base,
    tag_out, tag_in, disp, work, part, part_in, shrink, delta, delta_in,
    cache_sem, load_sem, pool_sem, q_sem, pa_send, pa_recv, pb_send, pb_recv, back_send, back_recv,
    hop_y_send, hop_y_recv, y_send, y_recv, hop_z_send, hop_z_recv, z_send, z_recv, a_send, a_recv, b_send, b_recv,
    tag_send, tag_recv, disp_send, disp_recv, part_send, part_recv, shr_send, shr_recv, del_send, del_recv,
):
    steps, rows, width = out.shape
    half = rows // 2
    heads = width // HD
    per_request = 2 * heads * steps
    total_rows = steps * rows
    part_width = width // 2
    bits = n_tp.bit_length() - 1
    cap_bits = CAP.bit_length() - 1

    rep = lax.axis_index("rep")
    t = lax.axis_index("tp")
    y, z = lax.div(t, side), lax.rem(t, side)
    member, group = lax.rem(t, 2), lax.div(t, 2)
    partner = t + 1 - 2 * member
    mine = pl.multiple_of(member * half, half)
    other = pl.multiple_of((1 - member) * half, half)

    def tp_peer(k):
        dy, dz = lax.div(k, side), lax.rem(k, side)
        return lax.rem(y + dy, side) * side + lax.rem(z + dz, side)

    chip, core = lax.div(rep, 2), lax.rem(rep, 2)
    chips = n_rep // 2

    def rep_peer(k):
        m, f = lax.div(k, 2), lax.rem(k, 2)
        return lax.rem(chip + m, chips) * 2 + lax.rem(core + f, 2)

    def remote(src, dst, send, recv, device):
        return pltpu.make_async_remote_copy(
            src_ref=src, dst_ref=dst, send_sem=send, recv_sem=recv, device_id=device, device_id_type=MESH
        )

    def over(low, high, body):
        def run(k, carry):
            body(k)
            return carry

        lax.fori_loop(low, high, run, 0)

    load_q = pltpu.make_async_copy(queries.at[:, pl.ds(mine, half), :], q_own, load_sem.at[0])
    load_fresh = pltpu.make_async_copy(
        new_kv.at[:, pl.ds(mine, half), pl.ds(pl.multiple_of(group * 2 * HD, 2 * HD), 2 * HD)], fresh, load_sem.at[1]
    )
    load_w = pltpu.make_async_copy(weight, w_buf, load_sem.at[2])

    def load_cache(c):
        span = pl.ds(c * KV_CHUNK, KV_CHUNK)
        return pltpu.make_async_copy(kv_cache.at[span], cache.at[span], cache_sem.at[c])

    def load_pool(p):
        span = pl.ds(pl.multiple_of(p * width, width), width)
        return pltpu.make_async_copy(panels.at[0, span, :], pool.at[p], pool_sem.at[p])

    barrier = pltpu.get_barrier_semaphore()
    over(1, n_tp, lambda k: pl.semaphore_signal(barrier, inc=1, device_id=(rep, tp_peer(k)), device_id_type=MESH))
    over(1, n_rep, lambda k: pl.semaphore_signal(barrier, inc=1, device_id=(rep_peer(k), t), device_id_type=MESH))
    load_q.start()
    over(0, n_tp, lambda p: load_pool(p).start())
    load_fresh.start()
    over(0, half // KV_CHUNK, lambda c: load_cache(c).start())
    load_w.start()
    pl.semaphore_wait(barrier, n_tp + n_rep - 2)

    swap_q = remote(queries.at[:, pl.ds(other, half), :], q_in, q_sem.at[0], q_sem.at[1], (rep, partner))
    swap_q.start()

    half_width = width // 2
    low_half = iota((half_width, LANES), 1) < RANK

    def pack(p):
        load_pool(p).wait()
        top = pool[p, :half_width, :].astype(F32)
        bottom = pool[p, half_width:, :].astype(F32)
        pack_a[p] = jnp.where(low_half, top, pltpu.roll(bottom, RANK, 1)).astype(BF16)
        pack_b[p] = jnp.where(low_half, pltpu.roll(top, RANK, 1), bottom).astype(BF16)

    pan_cols = pl.ds(pl.multiple_of(t * LANES, LANES), LANES)

    def send_a(k):
        peer = tp_peer(k)
        return remote(pack_a.at[peer], pan_a.at[:, pan_cols], pa_send.at[k], pa_recv.at[k], (rep, peer))

    def send_b(k):
        peer = tp_peer(k)
        return remote(pack_b.at[peer], pan_b.at[:, pan_cols], pb_send.at[k], pb_recv.at[k], (rep, peer))

    pan_batches = panel_batches(side)

    def start_all(send, batch):
        for k in pan_batches[batch]:
            send(k).start()

    for k in pan_batches[0] + pan_batches[1]:
        pack(tp_peer(k))
        send_a(k).start()
    for k in pan_batches[2]:
        pack(tp_peer(k))
    pack(t)
    keep_a = pltpu.make_async_copy(pack_a.at[t], pan_a.at[:, pan_cols], load_sem.at[3])
    keep_b = pltpu.make_async_copy(pack_b.at[t], pan_b.at[:, pan_cols], load_sem.at[4])
    keep_a.start()
    keep_b.start()

    n_dest = n_rep * CAP
    n_adapters = owners.shape[1]
    diagonal = iota((rows, rows), 0) == iota((rows, rows), 1)
    earlier = jnp.where(iota((rows, rows), 1) < iota((rows, rows), 0), 1.0, 0.0).astype(BF16)
    dest = iota((rows, n_dest), 1)
    for s in range(steps):
        id_row = jnp.broadcast_to(ids[s : s + 1, :].astype(F32), (rows, rows))
        id_col = jnp.sum(jnp.where(diagonal, id_row, 0.0), axis=1, keepdims=True)
        found = iota((rows, n_adapters), 1).astype(F32) == id_col
        owner_row = jnp.broadcast_to(owners[...].astype(F32), (rows, n_adapters))
        slot = jnp.sum(jnp.where(found, owner_row, 0.0), axis=1, keepdims=True).astype(jnp.int32)
        holder = lax.shift_right_logical(slot, bits)
        goes = lax.shift_right_logical(dest, cap_bits) == holder
        rank = dot(earlier, jnp.where(goes, 1.0, 0.0).astype(BF16))
        here = goes & (rank == (dest & (CAP - 1)).astype(F32))
        place[s] = jnp.where(here, 1.0, 0.0).astype(BF16)
        tags[s] = jnp.where(iota((rows, LANES), 1) == (slot & (n_tp - 1)), 1.0, 0.0).astype(BF16)
    spread[...] = jnp.where(
        iota(spread.shape, 0) == lax.shift_right_logical(iota(spread.shape, 1), 7), 1.0, 0.0
    ).astype(BF16)

    for s in range(steps):
        sent = tn_dot(place[s], tags[s]).astype(BF16).reshape(n_rep, CAP, LANES)
        tag_out[:, s * CAP : (s + 1) * CAP, :] = sent

    def send_tag(k):
        peer = rep_peer(k)
        return remote(tag_out.at[peer], tag_in.at[rep], tag_send.at[k], tag_recv.at[k], (peer, t))

    over(1, n_rep, lambda k: send_tag(k).start())
    tag_in[rep] = tag_out[rep]

    load_q.wait()
    load_fresh.wait()
    swap_q.wait()
    for s in range(steps):
        for h in range(heads):
            cols = slice(h * HD, (h + 1) * HD)
            q_rows[pl.ds(h * steps + s, half, stride=per_request), :] = q_own[s, :, cols].astype(F32)
            q_rows[pl.ds((heads + h) * steps + s, half, stride=per_request), :] = q_in[s, :, cols].astype(F32)

    scale = 1.0 / math.sqrt(HD)

    def rows_of(i):
        return pl.ds(pl.multiple_of(i * per_request, per_request), per_request)

    def attend_chunk(c):
        load_cache(c).wait()
        block = [c * KV_CHUNK + j for j in range(KV_CHUNK)]
        step_of = iota((per_request, 1), 0) & (steps - 1)
        fresh_rows = fresh[...].reshape(steps * half, 2 * HD)
        scores, own = [], []
        for i in block:
            q = q_rows[rows_of(i), :].astype(BF16)
            scores.append(nt_dot(q, cache[i, :, :HD]))
            own.append(nt_dot(q, fresh_rows[:, :HD]))
        total = []
        for j, i in enumerate(block):
            limit = jnp.zeros((per_request, 1), jnp.int32)
            for s in range(steps):
                limit = jnp.where(step_of == s, lengths[s, mine + i], limit)
            cached = jnp.where(iota(scores[j].shape, 1) < limit, scores[j] * scale, MASKED)
            fresh_score = jnp.where(iota(own[j].shape, 1) == step_of * half + i, own[j] * scale, MASKED)
            top = jnp.maximum(
                jnp.max(cached, axis=1, keepdims=True), jnp.max(fresh_score, axis=1, keepdims=True)
            )
            cached = jnp.exp(cached - top)
            fresh_score = jnp.exp(fresh_score - top)
            total.append(jnp.sum(cached, axis=1, keepdims=True) + jnp.sum(fresh_score, axis=1, keepdims=True))
            scores[j] = cached.astype(BF16)
            own[j] = fresh_score.astype(BF16)
        for j, i in enumerate(block):
            mixed = dot(scores[j], cache[i, :, HD:]) + dot(own[j], fresh_rows[:, HD:])
            o_rows[rows_of(i), :] = mixed / total[j]

    quarter = half // 2

    def swap_back(part):
        span = pl.ds(pl.multiple_of(mine + part * quarter, quarter), quarter)
        return remote(
            attn_back.at[:, pl.ds(part * quarter, quarter), :], attn.at[:, span, :],
            back_send.at[part], back_recv.at[part], (rep, partner),
        )

    for part_of in range(2):
        chunks = quarter // KV_CHUNK
        over(part_of * chunks, (part_of + 1) * chunks, attend_chunk)
        first = part_of * quarter * per_request
        span = pl.ds(pl.multiple_of(mine + part_of * quarter, quarter), quarter)
        back = slice(part_of * quarter, (part_of + 1) * quarter)
        for s in range(steps):
            for h in range(heads):
                cols = slice(h * HD, (h + 1) * HD)
                far_heads = o_rows[pl.ds(first + (heads + h) * steps + s, quarter, stride=per_request), :]
                attn_back[s, back, cols] = far_heads.astype(BF16)
        swap_back(part_of).start()
        if part_of == 0:
            start_all(send_a, 2)
        for s in range(steps):
            for h in range(heads):
                cols = slice(h * HD, (h + 1) * HD)
                own_heads = o_rows[pl.ds(first + h * steps + s, quarter, stride=per_request), :]
                attn[s, span, cols] = own_heads.astype(BF16)
    for part_of in range(2):
        swap_back(part_of).wait_recv()

    for s in range(steps):
        span = slice(s * CAP, (s + 1) * CAP)
        routed = tn_dot(place[s], attn[s]).astype(BF16)
        disp[:, span, :] = routed.reshape(n_rep, CAP, width)

    def send_disp(k):
        peer = rep_peer(k)
        return remote(disp.at[peer], work.at[rep], disp_send.at[k], disp_recv.at[k], (peer, t))

    near_first = (0, 1, chips - 1, 2)
    for m in near_first:
        for f in range(2):
            if m or f:
                send_disp(2 * m + f).start()
    work[rep] = disp[rep]

    load_w.wait()

    def project(block, part):
        cols = pl.ds(pl.multiple_of(block * width + part * part_width, part_width), part_width)
        return dot(attn[...].reshape(total_rows, width), w_buf[:, cols])

    half_total = total_rows // 2
    halves = (slice(0, half_total), slice(half_total, total_rows))

    def at_y(d):
        return lax.rem(y + d, side) * side + z

    def at_z(d):
        return y * side + lax.rem(z + d, side)

    def hop_along_y(way, j):
        return remote(
            far_y.at[way, j], hop_y.at[way, j], hop_y_send.at[way, j], hop_y_recv.at[way, j],
            (rep, at_y((side - 1, 1)[way])),
        )

    def hop_along_z(way, j):
        return remote(
            far_z.at[way, j], hop_z.at[way, j], hop_z_send.at[way, j], hop_z_recv.at[way, j],
            (rep, at_z((side - 1, 1)[way])),
        )

    def along_y(way, j):
        return remote(
            near_y.at[way, j], in_y.at[way, j], y_send.at[way, j], y_recv.at[way, j], (rep, at_y((side - 1, 1)[way]))
        )

    def along_z(way, j):
        return remote(
            near_z.at[way, j], in_z.at[way, j], z_send.at[way, j], z_recv.at[way, j], (rep, at_z((side - 1, 1)[way]))
        )

    def far_terms(j):
        to_z = lax.rem(z + 1 + j, side)
        to_y = lax.rem(y + 1 + j, side)
        term = project(lax.rem(y + 2, side) * side + to_z, 0).astype(BF16)
        for way in range(2):
            far_y[way, j] = term[halves[way]]
            hop_along_y(way, j).start()
        term = project(to_y * side + lax.rem(z + 2, side), 1).astype(BF16)
        for way in range(2):
            far_z[way, j] = term[halves[way]]
            hop_along_z(way, j).start()

    def near_terms(j):
        to_z = lax.rem(z + 1 + j, side)
        to_y = lax.rem(y + 1 + j, side)
        for way in range(2):
            d = (side - 1, 1)[way]
            term = project(lax.rem(y + d, side) * side + to_z, 0)
            near_y[way, j, halves[1 - way], :] = term[halves[1 - way]].astype(BF16)
            hop_along_y(way, j).wait_recv()
            near_y[way, j, halves[way], :] = (term[halves[way]] + hop_y[way, j].astype(F32)).astype(BF16)
            along_y(way, j).start()
            term = project(to_y * side + lax.rem(z + d, side), 1)
            near_z[way, j, halves[1 - way], :] = term[halves[1 - way]].astype(BF16)
            hop_along_z(way, j).wait_recv()
            near_z[way, j, halves[way], :] = (term[halves[way]] + hop_z[way, j].astype(F32)).astype(BF16)
            along_z(way, j).start()
        own_y[j] = project(y * side + to_z, 0)
        own_z[j] = project(to_y * side + z, 1)

    over(0, side, far_terms)
    start_all(send_b, 0)

    work_rows = n_rep * steps * CAP
    packed_rows = work_rows // 2
    tile = 2 * steps * CAP
    low_lanes = iota((tile, LANES), 1) < RANK
    low_all = (iota((tile, n_tp * LANES), 1) & (LANES - 1)) < RANK

    def masks(source):
        return dot(tag_in[pl.ds(2 * source, 2)].reshape(tile, LANES), spread[...])

    def packed(source):
        block = lax.rem(source, chips // 2)
        return pl.ds(pl.multiple_of(block * tile, tile), tile), source >= chips // 2

    over(1, n_rep, lambda k: send_tag(k).wait_recv())
    keep_a.wait()
    over(1, n_tp, lambda k: send_a(k).wait_recv())
    for order, m in enumerate(near_first):
        for f in range(2):
            if m or f:
                send_disp(2 * m + f).wait_recv()
        source = lax.rem(chip + chips - m, chips)
        x = work[pl.ds(2 * source, 2)].reshape(tile, width)
        products = jnp.where(
            low_all, dot(x[:, :half_width], pan_a[...]), dot(x[:, half_width:], pan_a[...])
        ) * masks(source)
        total = products[:, :LANES]
        for a in range(1, n_tp):
            total = total + products[:, a * LANES : (a + 1) * LANES]
        total = total + pltpu.roll(total, RANK, 1)
        place_rows, upper = packed(source)
        if order < 2:
            part[place_rows, :] = total
        else:
            part[place_rows, :] = jnp.where(low_lanes != upper, total, part[place_rows, :])

    slab = packed_rows // n_tp

    def slab_of(device):
        return pl.ds(pl.multiple_of(device * slab, slab), slab)

    def send_part(k):
        peer = tp_peer(k)
        return remote(part.at[slab_of(peer)], part_in.at[k], part_send.at[k], part_recv.at[k], (rep, peer))

    over(1, n_tp, lambda k: send_part(k).start())
    start_all(send_b, 1)
    start_all(send_b, 2)

    def forward_y(j):
        device = (rep, y * side + lax.rem(z + 1 + j, side))
        return remote(fwd_a.at[j], got_a.at[j], a_send.at[j], a_recv.at[j], device)

    def forward_z(j):
        device = (rep, lax.rem(y + 1 + j, side) * side + z)
        return remote(fwd_b.at[j], got_b.at[j], b_send.at[j], b_recv.at[j], device)

    def gathered(own, arrived, copy, j):
        total = own[j]
        for way in range(2):
            copy(way, j).wait_recv()
            total = total + arrived[way, j].astype(F32)
        return total

    def second_stage(j):
        fwd_a[j] = gathered(own_y, in_y, along_y, j).astype(BF16)
        forward_y(j).start()
        fwd_b[j] = gathered(own_z, in_z, along_z, j).astype(BF16)
        forward_z(j).start()

    over(1, n_tp, lambda k: send_part(k).wait_recv())
    total = part[slab_of(t), :]
    for k in range(1, n_tp):
        total = total + part_in[k]
    shrink[slab_of(t), :] = total.astype(BF16)

    def send_shrink(k):
        peer = tp_peer(k)
        return remote(shrink.at[slab_of(t)], shrink.at[slab_of(t)], shr_send.at[k], shr_recv.at[k], (rep, peer))

    over(1, n_tp, lambda k: send_shrink(k).start())
    over(0, side, near_terms)

    over(1, n_tp, lambda k: send_shrink(k).wait_recv())

    keep_b.wait()
    over(1, n_tp, lambda k: send_b(k).wait_recv())

    def send_delta(k):
        peer = rep_peer(k)
        return remote(delta.at[peer], delta_in.at[rep], del_send.at[k], del_recv.at[k], (peer, t))

    for m in near_first[::-1]:
        source = lax.rem(chip + m, chips)
        place_rows, upper = packed(source)
        shrunk = shrink[place_rows, :].astype(F32)
        turned = pltpu.roll(shrunk, RANK, 1)
        in_low = jnp.where(low_lanes, jnp.where(upper, turned, shrunk), 0.0)
        in_high = jnp.where(low_lanes, 0.0, jnp.where(upper, shrunk, turned))
        mask = masks(source)
        for side_of, placed in enumerate((in_low, in_high)):
            picked = (mask * jnp.concatenate([placed] * n_tp, axis=1)).astype(BF16)
            result = nt_dot(picked, pan_b[...]).astype(BF16)
            cols = slice(side_of * half_width, (side_of + 1) * half_width)
            delta[pl.ds(2 * source, 2), :, cols] = result.reshape(2, steps * CAP, half_width)
        for f in range(2):
            if m or f:
                send_delta(2 * m + f).start()
    delta_in[rep] = delta[rep]
    over(0, side - 1, second_stage)

    last = side - 1
    base[:, :part_width] = gathered(own_y, in_y, along_y, last)
    base[:, part_width:] = gathered(own_z, in_z, along_z, last)
    for j in range(last):
        forward_y(j).wait_recv()
        base[:, :part_width] += got_a[j].astype(F32)
        forward_z(j).wait_recv()
        base[:, part_width:] += got_b[j].astype(F32)

    over(1, n_rep, lambda k: send_delta(k).wait_recv())
    for s in range(steps):
        rows_in = delta_in[:, s * CAP : (s + 1) * CAP, :].reshape(n_dest, width)
        update = dot(place[s], rows_in)
        out[s] = (base[s * rows : (s + 1) * rows, :] + ADAPTER_SCALING * update).astype(BF16)

    def drain_tp(k):
        send_a(k).wait_send()
        send_b(k).wait_send()
        send_part(k).wait_send()
        send_shrink(k).wait_send()

    def drain_rep(k):
        send_tag(k).wait_send()
        send_disp(k).wait_send()
        send_delta(k).wait_send()

    def drain_sums(j):
        for way in range(2):
            hop_along_y(way, j).wait_send()
            hop_along_z(way, j).wait_send()
            along_y(way, j).wait_send()
            along_z(way, j).wait_send()

    def drain_forward(j):
        forward_y(j).wait_send()
        forward_z(j).wait_send()

    for part_of in range(2):
        swap_back(part_of).wait_send()
    over(1, n_tp, drain_tp)
    over(1, n_rep, drain_rep)
    over(0, side, drain_sums)
    over(0, side - 1, drain_forward)


def shards(n_rep, n_tp, queries, new_kv, kv_cache, lengths, adapter_ids, owner_slot, panels, out_weight):
    side = math.isqrt(n_tp)
    steps, rows, width = queries.shape
    half = rows // 2
    heads = width // HD
    total = steps * rows
    part = width // 2
    per_request = 2 * heads * steps
    work_rows = n_rep * steps * CAP
    dma = pltpu.SemaphoreType.DMA
    vmem = pltpu.VMEM
    hop = side - 1
    scratch = [
        vmem((steps, half, width), BF16),
        vmem((steps, half, width), BF16),
        vmem((half * per_request, HD), F32),
        vmem((half * per_request, HD), F32),
        vmem((steps, half, 2 * HD), BF16),
        vmem(kv_cache.shape, BF16),
        vmem(out_weight.shape, BF16),
        vmem((n_tp, width, LANES), BF16),
        vmem((n_tp, width // 2, LANES), BF16),
        vmem((n_tp, width // 2, LANES), BF16),
        vmem((width // 2, n_tp * LANES), BF16),
        vmem((width // 2, n_tp * LANES), BF16),
        vmem((LANES, n_tp * LANES), BF16),
        vmem((steps, rows, width), BF16),
        vmem((steps, half, width), BF16),
        vmem((steps, rows, LANES), BF16),
        vmem((steps, rows, n_rep * CAP), BF16),
        vmem((2, side, total // 2, part), BF16),
        vmem((2, side, total // 2, part), BF16),
        vmem((2, side, total, part), BF16),
        vmem((2, side, total, part), BF16),
        vmem((side, total, part), F32),
        vmem((2, side, total // 2, part), BF16),
        vmem((2, side, total // 2, part), BF16),
        vmem((2, side, total, part), BF16),
        vmem((2, side, total, part), BF16),
        vmem((side, total, part), F32),
        vmem((hop, total, part), BF16),
        vmem((hop, total, part), BF16),
        vmem((hop, total, part), BF16),
        vmem((hop, total, part), BF16),
        vmem((total, width), F32),
        vmem((n_rep, steps * CAP, LANES), BF16),
        vmem((n_rep, steps * CAP, LANES), BF16),
        vmem((n_rep, steps * CAP, width), BF16),
        vmem((n_rep, steps * CAP, width), BF16),
        vmem((work_rows // 2, LANES), F32),
        vmem((n_tp, work_rows // 2 // n_tp, LANES), F32),
        vmem((work_rows // 2, LANES), BF16),
        vmem((n_rep, steps * CAP, width), BF16),
        vmem((n_rep, steps * CAP, width), BF16),
        dma((half // KV_CHUNK,)),
        dma((5,)),
        dma((n_tp,)),
        dma((2,)),
        dma((n_tp,)), dma((n_tp,)),
        dma((n_tp,)), dma((n_tp,)),
        dma((2,)), dma((2,)),
        dma((2, side)), dma((2, side)),
        dma((2, side)), dma((2, side)),
        dma((2, side)), dma((2, side)),
        dma((2, side)), dma((2, side)),
        dma((hop,)), dma((hop,)),
        dma((hop,)), dma((hop,)),
        dma((n_rep,)), dma((n_rep,)),
        dma((n_rep,)), dma((n_rep,)),
        dma((n_tp,)), dma((n_tp,)),
        dma((n_tp,)), dma((n_tp,)),
        dma((n_rep,)), dma((n_rep,)),
    ]
    hbm = pl.BlockSpec(memory_space=pl.ANY)
    in_vmem = pl.BlockSpec(memory_space=pltpu.VMEM)
    in_smem = pl.BlockSpec(memory_space=pltpu.SMEM)
    return pl.pallas_call(
        functools.partial(kernel, n_rep, n_tp, side),
        out_shape=jax.ShapeDtypeStruct(queries.shape, BF16),
        in_specs=[hbm, hbm, hbm, in_smem, in_vmem, in_vmem, hbm, hbm],
        out_specs=in_vmem,
        scratch_shapes=scratch,
        compiler_params=pltpu.CompilerParams(
            collective_id=0, has_side_effects=True, vmem_limit_bytes=56 * 1024 * 1024
        ),
        cost_estimate=pl.CostEstimate(
            flops=5_000_000_000, bytes_accessed=20_000_000, transcendentals=600_000
        ),
    )(queries, new_kv, kv_cache, lengths, adapter_ids, owner_slot.reshape(1, -1), panels, out_weight)


def solution(mesh):
    placed = (
        P(None, "rep", "tp"),
        P(None, "rep", None),
        P("rep", None, "tp"),
        P(None, "rep"),
        P(None, "rep"),
        P(),
        P(("rep", "tp"), None, None),
        P("tp", None),
    )
    return jax.shard_map(
        functools.partial(shards, mesh.shape["rep"], mesh.shape["tp"]),
        mesh=mesh, in_specs=placed, out_specs=P(None, "rep", "tp"), check_vma=False,
    )
```

```python
import functools
import math

import jax
import jax.numpy as jnp
from jax import lax
from jax.experimental import pallas as pl
from jax.experimental.pallas import tpu as pltpu
from jax.sharding import PartitionSpec as P

MESH = pl.DeviceIdType.MESH
F32 = jnp.float32
BF16 = jnp.bfloat16

HD = 128
RANK = 64
CAP = 16
LANES = 128
KV_CHUNK = 8
ADAPTER_SCALING = 2.0
MASKED = -1e30


def nt_dot(a, b):
    return lax.dot_general(a, b, (((1,), (1,)), ((), ())), preferred_element_type=F32)


def tn_dot(a, b):
    return lax.dot_general(a, b, (((0,), (0,)), ((), ())), preferred_element_type=F32)


def dot(a, b):
    return jnp.dot(a, b, preferred_element_type=F32)


def iota(shape, dim):
    return lax.broadcasted_iota(jnp.int32, shape, dim)


def panel_batches(side):
    def far(v):
        return min(v, side - v)

    offsets = [(dy, dz) for dy in range(side) for dz in range(side) if dy or dz]
    batches = [[], [], []]
    for dy, dz in offsets:
        if far(dy) == far(dz):
            batches[0].append((far(dy), dy, dz))
        elif far(dy) + far(dz) == 2:
            batches[1].append((0, dy, dz))
        else:
            batches[2].append((-far(dy) - far(dz), dy, dz))
    return [[dy * side + dz for _, dy, dz in sorted(batch)] for batch in batches]


def kernel(
    n_rep, n_tp, side,
    queries, new_kv, kv_cache, lengths, ids, owners, panels, weight,
    out,
    q_own, q_in, q_rows, o_rows, fresh, cache, w_buf, pool, pack_a, pack_b, pan_a, pan_b, spread, attn, attn_back, tags, place,
    far_y, hop_y, near_y, in_y, own_y, far_z, hop_z, near_z, in_z, own_z, fwd_a, got_a, fwd_b, got_b, base,
    tag_out, tag_in, disp, work, part, part_in, shrink, delta, delta_in,
    cache_sem, load_sem, pool_sem, q_sem, pa_send, pa_recv, pb_send, pb_recv, back_send, back_recv,
    hop_y_send, hop_y_recv, y_send, y_recv, hop_z_send, hop_z_recv, z_send, z_recv, a_send, a_recv, b_send, b_recv,
    tag_send, tag_recv, disp_send, disp_recv, part_send, part_recv, shr_send, shr_recv, del_send, del_recv,
):
    steps, rows, width = out.shape
    half = rows // 2
    heads = width // HD
    per_request = 2 * heads * steps
    total_rows = steps * rows
    part_width = width // 2
    bits = n_tp.bit_length() - 1
    cap_bits = CAP.bit_length() - 1

    rep = lax.axis_index("rep")
    t = lax.axis_index("tp")
    y, z = lax.div(t, side), lax.rem(t, side)
    member, group = lax.rem(t, 2), lax.div(t, 2)
    partner = t + 1 - 2 * member
    mine = pl.multiple_of(member * half, half)
    other = pl.multiple_of((1 - member) * half, half)

    def tp_peer(k):
        dy, dz = lax.div(k, side), lax.rem(k, side)
        return lax.rem(y + dy, side) * side + lax.rem(z + dz, side)

    chip, core = lax.div(rep, 2), lax.rem(rep, 2)
    chips = n_rep // 2

    def rep_peer(k):
        m, f = lax.div(k, 2), lax.rem(k, 2)
        return lax.rem(chip + m, chips) * 2 + lax.rem(core + f, 2)

    def remote(src, dst, send, recv, device):
        return pltpu.make_async_remote_copy(
            src_ref=src, dst_ref=dst, send_sem=send, recv_sem=recv, device_id=device, device_id_type=MESH
        )

    def landed(region, sem):
        pltpu.make_async_copy(region, region, sem.at[0]).wait()

    def over(low, high, body):
        def run(k, carry):
            body(k)
            return carry

        lax.fori_loop(low, high, run, 0)

    load_q = pltpu.make_async_copy(queries.at[:, pl.ds(mine, half), :], q_own, load_sem.at[0])
    load_fresh = pltpu.make_async_copy(
        new_kv.at[:, pl.ds(mine, half), pl.ds(pl.multiple_of(group * 2 * HD, 2 * HD), 2 * HD)], fresh, load_sem.at[1]
    )
    load_w = pltpu.make_async_copy(weight, w_buf, load_sem.at[2])

    def load_cache(c):
        span = pl.ds(c * KV_CHUNK, KV_CHUNK)
        return pltpu.make_async_copy(kv_cache.at[span], cache.at[span], cache_sem.at[c])

    def load_pool(p):
        span = pl.ds(pl.multiple_of(p * width, width), width)
        return pltpu.make_async_copy(panels.at[0, span, :], pool.at[p], pool_sem.at[p])

    barrier = pltpu.get_barrier_semaphore()
    for k in range(1, n_tp):
        pl.semaphore_signal(barrier, inc=1, device_id=(rep, tp_peer(k)), device_id_type=MESH)
    for k in range(1, n_rep):
        pl.semaphore_signal(barrier, inc=1, device_id=(rep_peer(k), t), device_id_type=MESH)
    over(0, n_tp, lambda p: load_pool(p).start())
    load_q.start()
    load_fresh.start()
    over(0, half // KV_CHUNK, lambda c: load_cache(c).start())
    load_w.start()
    half_width = width // 2
    low_half = iota((half_width, LANES), 1) < RANK

    def pack(p):
        load_pool(p).wait()
        top = pool[p, :half_width, :].astype(F32)
        bottom = pool[p, half_width:, :].astype(F32)
        pack_a[p] = jnp.where(low_half, top, pltpu.roll(bottom, RANK, 1)).astype(BF16)
        pack_b[p] = jnp.where(low_half, pltpu.roll(top, RANK, 1), bottom).astype(BF16)

    pan_cols = pl.ds(pl.multiple_of(t * LANES, LANES), LANES)

    def send_a(k):
        peer = tp_peer(k)
        return remote(pack_a.at[peer], pan_a.at[:, pan_cols], pa_send.at[0], pa_recv.at[0], (rep, peer))

    def send_b(k):
        peer = tp_peer(k)
        return remote(pack_b.at[peer], pan_b.at[:, pan_cols], pb_send.at[0], pb_recv.at[0], (rep, peer))

    pan_batches = panel_batches(side)
    spread_out = pan_batches[0] + pan_batches[1] + pan_batches[2]

    def start_all(send, batch):
        for k in pan_batches[batch]:
            send(k).start()

    over(0, n_tp, pack)

    pl.semaphore_wait(barrier, n_tp + n_rep - 2)

    swap_q = remote(queries.at[:, pl.ds(other, half), :], q_in, q_sem.at[0], q_sem.at[1], (rep, partner))
    swap_q.start()

    for k in pan_batches[0] + pan_batches[1] + pan_batches[2]:
        send_a(k).start()
    keep_a = pltpu.make_async_copy(pack_a.at[t], pan_a.at[:, pan_cols], load_sem.at[3])
    keep_b = pltpu.make_async_copy(pack_b.at[t], pan_b.at[:, pan_cols], load_sem.at[4])
    keep_a.start()
    keep_b.start()

    n_dest = n_rep * CAP
    n_adapters = owners.shape[1]
    diagonal = iota((rows, rows), 0) == iota((rows, rows), 1)
    earlier = jnp.where(iota((rows, rows), 1) < iota((rows, rows), 0), 1.0, 0.0).astype(BF16)
    dest = iota((rows, n_dest), 1)
    for s in range(steps):
        id_row = jnp.broadcast_to(ids[s : s + 1, :].astype(F32), (rows, rows))
        id_col = jnp.sum(jnp.where(diagonal, id_row, 0.0), axis=1, keepdims=True)
        found = iota((rows, n_adapters), 1).astype(F32) == id_col
        owner_row = jnp.broadcast_to(owners[...].astype(F32), (rows, n_adapters))
        slot = jnp.sum(jnp.where(found, owner_row, 0.0), axis=1, keepdims=True).astype(jnp.int32)
        holder = lax.shift_right_logical(slot, bits)
        goes = lax.shift_right_logical(dest, cap_bits) == holder
        rank = dot(earlier, jnp.where(goes, 1.0, 0.0).astype(BF16))
        here = goes & (rank == (dest & (CAP - 1)).astype(F32))
        place[s] = jnp.where(here, 1.0, 0.0).astype(BF16)
        tags[s] = jnp.where(iota((rows, LANES), 1) == (slot & (n_tp - 1)), 1.0, 0.0).astype(BF16)
    spread[...] = jnp.where(
        iota(spread.shape, 0) == lax.shift_right_logical(iota(spread.shape, 1), 7), 1.0, 0.0
    ).astype(BF16)

    for s in range(steps):
        sent = tn_dot(place[s], tags[s]).astype(BF16).reshape(n_rep, CAP, LANES)
        tag_out[:, s * CAP : (s + 1) * CAP, :] = sent

    def send_tag(k):
        peer = rep_peer(k)
        return remote(tag_out.at[peer], tag_in.at[rep], tag_send.at[0], tag_recv.at[0], (peer, t))

    for k in range(1, n_rep):
        send_tag(k).start()
    tag_in[rep] = tag_out[rep]

    load_q.wait()
    load_fresh.wait()
    swap_q.wait()
    for s in range(steps):
        for h in range(heads):
            cols = slice(h * HD, (h + 1) * HD)
            q_rows[pl.ds(h * steps + s, half, stride=per_request), :] = q_own[s, :, cols].astype(F32)
            q_rows[pl.ds((heads + h) * steps + s, half, stride=per_request), :] = q_in[s, :, cols].astype(F32)

    scale = 1.0 / math.sqrt(HD)

    def rows_of(i):
        return pl.ds(pl.multiple_of(i * per_request, per_request), per_request)

    def attend_chunk(c):
        load_cache(c).wait()
        block = [c * KV_CHUNK + j for j in range(KV_CHUNK)]
        step_of = iota((per_request, 1), 0) & (steps - 1)
        fresh_rows = fresh[...].reshape(steps * half, 2 * HD)
        scores, own = [], []
        for i in block:
            q = q_rows[rows_of(i), :].astype(BF16)
            scores.append(nt_dot(q, cache[i, :, :HD]))
            own.append(nt_dot(q, fresh_rows[:, :HD]))
        total = []
        for j, i in enumerate(block):
            limit = jnp.zeros((per_request, 1), jnp.int32)
            for s in range(steps):
                limit = jnp.where(step_of == s, lengths[s, mine + i], limit)
            cached = jnp.where(iota(scores[j].shape, 1) < limit, scores[j] * scale, MASKED)
            fresh_score = jnp.where(iota(own[j].shape, 1) == step_of * half + i, own[j] * scale, MASKED)
            top = jnp.maximum(
                jnp.max(cached, axis=1, keepdims=True), jnp.max(fresh_score, axis=1, keepdims=True)
            )
            cached = jnp.exp(cached - top)
            fresh_score = jnp.exp(fresh_score - top)
            total.append(jnp.sum(cached, axis=1, keepdims=True) + jnp.sum(fresh_score, axis=1, keepdims=True))
            scores[j] = cached.astype(BF16)
            own[j] = fresh_score.astype(BF16)
        for j, i in enumerate(block):
            mixed = dot(scores[j], cache[i, :, HD:]) + dot(own[j], fresh_rows[:, HD:])
            o_rows[rows_of(i), :] = mixed / total[j]

    quarter = half // 2

    def swap_back(part):
        span = pl.ds(pl.multiple_of(mine + part * quarter, quarter), quarter)
        return remote(
            attn_back.at[:, pl.ds(part * quarter, quarter), :], attn.at[:, span, :],
            back_send.at[part], back_recv.at[part], (rep, partner),
        )

    for part_of in range(2):
        chunks = quarter // KV_CHUNK
        over(part_of * chunks, (part_of + 1) * chunks, attend_chunk)
        first = part_of * quarter * per_request
        span = pl.ds(pl.multiple_of(mine + part_of * quarter, quarter), quarter)
        back = slice(part_of * quarter, (part_of + 1) * quarter)
        for s in range(steps):
            for h in range(heads):
                cols = slice(h * HD, (h + 1) * HD)
                far_heads = o_rows[pl.ds(first + (heads + h) * steps + s, quarter, stride=per_request), :]
                attn_back[s, back, cols] = far_heads.astype(BF16)
        swap_back(part_of).start()
        for s in range(steps):
            for h in range(heads):
                cols = slice(h * HD, (h + 1) * HD)
                own_heads = o_rows[pl.ds(first + h * steps + s, quarter, stride=per_request), :]
                attn[s, span, cols] = own_heads.astype(BF16)
    for part_of in range(2):
        swap_back(part_of).wait_recv()

    for s in range(steps):
        span = slice(s * CAP, (s + 1) * CAP)
        routed = tn_dot(place[s], attn[s]).astype(BF16)
        disp[:, span, :] = routed.reshape(n_rep, CAP, width)

    def send_disp(k):
        peer = rep_peer(k)
        return remote(disp.at[peer], work.at[rep], disp_send.at[0], disp_recv.at[k], (peer, t))

    near_first = (0, 1, chips - 1, 2)
    for m in near_first:
        for f in range(2):
            if m or f:
                send_disp(2 * m + f).start()
    work[rep] = disp[rep]

    load_w.wait()

    def project(block, part):
        cols = pl.ds(pl.multiple_of(block * width + part * part_width, part_width), part_width)
        return dot(attn[...].reshape(total_rows, width), w_buf[:, cols])

    half_total = total_rows // 2
    halves = (slice(0, half_total), slice(half_total, total_rows))

    def at_y(d):
        return lax.rem(y + d, side) * side + z

    def at_z(d):
        return y * side + lax.rem(z + d, side)

    def hop_along_y(way, j):
        return remote(
            far_y.at[way, j], hop_y.at[way, j], hop_y_send.at[0], hop_y_recv.at[way, j],
            (rep, at_y((side - 1, 1)[way])),
        )

    def hop_along_z(way, j):
        return remote(
            far_z.at[way, j], hop_z.at[way, j], hop_z_send.at[0], hop_z_recv.at[way, j],
            (rep, at_z((side - 1, 1)[way])),
        )

    def along_y(way, j):
        return remote(
            near_y.at[way, j], in_y.at[way, j], y_send.at[0], y_recv.at[way, j], (rep, at_y((side - 1, 1)[way]))
        )

    def along_z(way, j):
        return remote(
            near_z.at[way, j], in_z.at[way, j], z_send.at[0], z_recv.at[way, j], (rep, at_z((side - 1, 1)[way]))
        )

    def far_terms(j):
        to_z = lax.rem(z + 1 + j, side)
        to_y = lax.rem(y + 1 + j, side)
        term = project(lax.rem(y + 2, side) * side + to_z, 0).astype(BF16)
        for way in range(2):
            far_y[way, j] = term[halves[way]]
            hop_along_y(way, j).start()
        term = project(to_y * side + lax.rem(z + 2, side), 1).astype(BF16)
        for way in range(2):
            far_z[way, j] = term[halves[way]]
            hop_along_z(way, j).start()

    def near_terms(j):
        to_z = lax.rem(z + 1 + j, side)
        to_y = lax.rem(y + 1 + j, side)
        for way in range(2):
            d = (side - 1, 1)[way]
            term = project(lax.rem(y + d, side) * side + to_z, 0)
            near_y[way, j, halves[1 - way], :] = term[halves[1 - way]].astype(BF16)
            hop_along_y(way, j).wait_recv()
            near_y[way, j, halves[way], :] = (term[halves[way]] + hop_y[way, j].astype(F32)).astype(BF16)
            along_y(way, j).start()
            term = project(to_y * side + lax.rem(z + d, side), 1)
            near_z[way, j, halves[1 - way], :] = term[halves[1 - way]].astype(BF16)
            hop_along_z(way, j).wait_recv()
            near_z[way, j, halves[way], :] = (term[halves[way]] + hop_z[way, j].astype(F32)).astype(BF16)
            along_z(way, j).start()
        own_y[j] = project(y * side + to_z, 0)
        own_z[j] = project(to_y * side + z, 1)

    over(0, side, far_terms)
    start_all(send_b, 0)

    work_rows = n_rep * steps * CAP
    packed_rows = work_rows // 2
    tile = 2 * steps * CAP
    low_lanes = iota((tile, LANES), 1) < RANK
    low_all = (iota((tile, n_tp * LANES), 1) & (LANES - 1)) < RANK

    def masks(source):
        return dot(tag_in[pl.ds(2 * source, 2)].reshape(tile, LANES), spread[...])

    def packed(source):
        block = lax.rem(source, chips // 2)
        return pl.ds(pl.multiple_of(block * tile, tile), tile), source >= chips // 2

    landed(tag_in.at[pl.ds(0, n_rep - 1)], tag_recv)
    keep_a.wait()
    landed(pan_a.at[:, pl.ds(0, (n_tp - 1) * LANES)], pa_recv)
    for order, m in enumerate(near_first):
        for f in range(2):
            if m or f:
                send_disp(2 * m + f).wait_recv()
        source = lax.rem(chip + chips - m, chips)
        x = work[pl.ds(2 * source, 2)].reshape(tile, width)
        products = jnp.where(
            low_all, dot(x[:, :half_width], pan_a[...]), dot(x[:, half_width:], pan_a[...])
        ) * masks(source)
        total = products[:, :LANES]
        for a in range(1, n_tp):
            total = total + products[:, a * LANES : (a + 1) * LANES]
        total = total + pltpu.roll(total, RANK, 1)
        place_rows, upper = packed(source)
        if order < 2:
            part[place_rows, :] = total
        else:
            part[place_rows, :] = jnp.where(low_lanes != upper, total, part[place_rows, :])

    slab = packed_rows // n_tp

    def slab_of(device):
        return pl.ds(pl.multiple_of(device * slab, slab), slab)

    def send_part(k):
        peer = tp_peer(k)
        return remote(part.at[slab_of(peer)], part_in.at[k], part_send.at[0], part_recv.at[0], (rep, peer))

    for k in spread_out:
        send_part(k).start()
    start_all(send_b, 1)
    start_all(send_b, 2)

    def forward_y(j):
        device = (rep, y * side + lax.rem(z + 1 + j, side))
        return remote(fwd_a.at[j], got_a.at[j], a_send.at[0], a_recv.at[j], device)

    def forward_z(j):
        device = (rep, lax.rem(y + 1 + j, side) * side + z)
        return remote(fwd_b.at[j], got_b.at[j], b_send.at[0], b_recv.at[j], device)

    def gathered(own, arrived, copy, j):
        total = own[j]
        for way in range(2):
            copy(way, j).wait_recv()
            total = total + arrived[way, j].astype(F32)
        return total

    def second_stage(j):
        fwd_a[j] = gathered(own_y, in_y, along_y, j).astype(BF16)
        forward_y(j).start()
        fwd_b[j] = gathered(own_z, in_z, along_z, j).astype(BF16)
        forward_z(j).start()

    landed(part_in.at[pl.ds(1, n_tp - 1)], part_recv)
    total = part[slab_of(t), :]
    for k in range(1, n_tp):
        total = total + part_in[k]
    shrink[slab_of(t), :] = total.astype(BF16)

    def send_shrink(k):
        peer = tp_peer(k)
        return remote(shrink.at[slab_of(t)], shrink.at[slab_of(t)], shr_send.at[0], shr_recv.at[0], (rep, peer))

    for k in spread_out:
        send_shrink(k).start()
    over(0, side, near_terms)

    landed(shrink.at[pl.ds(0, (n_tp - 1) * slab)], shr_recv)

    keep_b.wait()
    landed(pan_b.at[:, pl.ds(0, (n_tp - 1) * LANES)], pb_recv)

    def send_delta(k):
        peer = rep_peer(k)
        return remote(delta.at[peer], delta_in.at[rep], del_send.at[0], del_recv.at[0], (peer, t))

    for m in near_first[::-1]:
        source = lax.rem(chip + m, chips)
        place_rows, upper = packed(source)
        shrunk = shrink[place_rows, :].astype(F32)
        turned = pltpu.roll(shrunk, RANK, 1)
        in_low = jnp.where(low_lanes, jnp.where(upper, turned, shrunk), 0.0)
        in_high = jnp.where(low_lanes, 0.0, jnp.where(upper, shrunk, turned))
        mask = masks(source)
        for side_of, placed in enumerate((in_low, in_high)):
            picked = (mask * jnp.concatenate([placed] * n_tp, axis=1)).astype(BF16)
            result = nt_dot(picked, pan_b[...]).astype(BF16)
            cols = slice(side_of * half_width, (side_of + 1) * half_width)
            delta[pl.ds(2 * source, 2), :, cols] = result.reshape(2, steps * CAP, half_width)
        for f in range(2):
            if m or f:
                send_delta(2 * m + f).start()
    delta_in[rep] = delta[rep]
    over(0, side - 1, second_stage)

    last = side - 1
    base[:, :part_width] = gathered(own_y, in_y, along_y, last)
    base[:, part_width:] = gathered(own_z, in_z, along_z, last)
    for j in range(last):
        forward_y(j).wait_recv()
        base[:, :part_width] += got_a[j].astype(F32)
        forward_z(j).wait_recv()
        base[:, part_width:] += got_b[j].astype(F32)

    landed(delta_in.at[pl.ds(0, n_rep - 1)], del_recv)
    for s in range(steps):
        rows_in = delta_in[:, s * CAP : (s + 1) * CAP, :].reshape(n_dest, width)
        update = dot(place[s], rows_in)
        out[s] = (base[s * rows : (s + 1) * rows, :] + ADAPTER_SCALING * update).astype(BF16)

    for part_of in range(2):
        swap_back(part_of).wait_send()
    landed(pack_a.at[pl.ds(0, n_tp - 1)], pa_send)
    landed(pack_b.at[pl.ds(0, n_tp - 1)], pb_send)
    landed(tag_out.at[pl.ds(0, n_rep - 1)], tag_send)
    landed(disp.at[pl.ds(0, n_rep - 1)], disp_send)
    landed(part_in.at[pl.ds(1, n_tp - 1)], part_send)
    landed(shrink.at[pl.ds(0, (n_tp - 1) * slab)], shr_send)
    landed(delta.at[pl.ds(0, n_rep - 1)], del_send)
    landed(far_y, hop_y_send)
    landed(far_z, hop_z_send)
    landed(near_y, y_send)
    landed(near_z, z_send)
    landed(fwd_a, a_send)
    landed(fwd_b, b_send)


def shards(n_rep, n_tp, queries, new_kv, kv_cache, lengths, adapter_ids, owner_slot, panels, out_weight):
    side = math.isqrt(n_tp)
    steps, rows, width = queries.shape
    half = rows // 2
    heads = width // HD
    total = steps * rows
    part = width // 2
    per_request = 2 * heads * steps
    work_rows = n_rep * steps * CAP
    dma = pltpu.SemaphoreType.DMA
    vmem = pltpu.VMEM
    hop = side - 1
    scratch = [
        vmem((steps, half, width), BF16),
        vmem((steps, half, width), BF16),
        vmem((half * per_request, HD), F32),
        vmem((half * per_request, HD), F32),
        vmem((steps, half, 2 * HD), BF16),
        vmem(kv_cache.shape, BF16),
        vmem(out_weight.shape, BF16),
        vmem((n_tp, width, LANES), BF16),
        vmem((n_tp, width // 2, LANES), BF16),
        vmem((n_tp, width // 2, LANES), BF16),
        vmem((width // 2, n_tp * LANES), BF16),
        vmem((width // 2, n_tp * LANES), BF16),
        vmem((LANES, n_tp * LANES), BF16),
        vmem((steps, rows, width), BF16),
        vmem((steps, half, width), BF16),
        vmem((steps, rows, LANES), BF16),
        vmem((steps, rows, n_rep * CAP), BF16),
        vmem((2, side, total // 2, part), BF16),
        vmem((2, side, total // 2, part), BF16),
        vmem((2, side, total, part), BF16),
        vmem((2, side, total, part), BF16),
        vmem((side, total, part), F32),
        vmem((2, side, total // 2, part), BF16),
        vmem((2, side, total // 2, part), BF16),
        vmem((2, side, total, part), BF16),
        vmem((2, side, total, part), BF16),
        vmem((side, total, part), F32),
        vmem((hop, total, part), BF16),
        vmem((hop, total, part), BF16),
        vmem((hop, total, part), BF16),
        vmem((hop, total, part), BF16),
        vmem((total, width), F32),
        vmem((n_rep, steps * CAP, LANES), BF16),
        vmem((n_rep, steps * CAP, LANES), BF16),
        vmem((n_rep, steps * CAP, width), BF16),
        vmem((n_rep, steps * CAP, width), BF16),
        vmem((work_rows // 2, LANES), F32),
        vmem((n_tp, work_rows // 2 // n_tp, LANES), F32),
        vmem((work_rows // 2, LANES), BF16),
        vmem((n_rep, steps * CAP, width), BF16),
        vmem((n_rep, steps * CAP, width), BF16),
        dma((half // KV_CHUNK,)),
        dma((5,)),
        dma((n_tp,)),
        dma((2,)),
        dma((1,)), dma((1,)),
        dma((1,)), dma((1,)),
        dma((2,)), dma((2,)),
        dma((1,)), dma((2, side)),
        dma((1,)), dma((2, side)),
        dma((1,)), dma((2, side)),
        dma((1,)), dma((2, side)),
        dma((1,)), dma((hop,)),
        dma((1,)), dma((hop,)),
        dma((1,)), dma((1,)),
        dma((1,)), dma((n_rep,)),
        dma((1,)), dma((1,)),
        dma((1,)), dma((1,)),
        dma((1,)), dma((1,)),
    ]
    hbm = pl.BlockSpec(memory_space=pl.ANY)
    in_vmem = pl.BlockSpec(memory_space=pltpu.VMEM)
    in_smem = pl.BlockSpec(memory_space=pltpu.SMEM)
    return pl.pallas_call(
        functools.partial(kernel, n_rep, n_tp, side),
        out_shape=jax.ShapeDtypeStruct(queries.shape, BF16),
        in_specs=[hbm, hbm, hbm, in_smem, in_vmem, in_vmem, hbm, hbm],
        out_specs=in_vmem,
        scratch_shapes=scratch,
        compiler_params=pltpu.CompilerParams(
            collective_id=0, has_side_effects=True, vmem_limit_bytes=56 * 1024 * 1024
        ),
        cost_estimate=pl.CostEstimate(
            flops=5_000_000_000, bytes_accessed=20_000_000, transcendentals=600_000
        ),
    )(queries, new_kv, kv_cache, lengths, adapter_ids, owner_slot.reshape(1, -1), panels, out_weight)


def solution(mesh):
    placed = (
        P(None, "rep", "tp"),
        P(None, "rep", None),
        P("rep", None, "tp"),
        P(None, "rep"),
        P(None, "rep"),
        P(),
        P(("rep", "tp"), None, None),
        P("tp", None),
    )
    return jax.shard_map(
        functools.partial(shards, mesh.shape["rep"], mesh.shape["tp"]),
        mesh=mesh, in_specs=placed, out_specs=P(None, "rep", "tp"), check_vma=False,
    )
```

```python
import functools
import math

import jax
import jax.numpy as jnp
from jax import lax
from jax.experimental import pallas as pl
from jax.experimental.pallas import tpu as pltpu
from jax.sharding import PartitionSpec as P

MESH = pl.DeviceIdType.MESH
F32 = jnp.float32
BF16 = jnp.bfloat16

HD = 128
RANK = 64
CAP = 16
LANES = 128
KV_CHUNK = 8
ADAPTER_SCALING = 2.0
MASKED = -1e30


def nt_dot(a, b):
    return lax.dot_general(a, b, (((1,), (1,)), ((), ())), preferred_element_type=F32)


def tn_dot(a, b):
    return lax.dot_general(a, b, (((0,), (0,)), ((), ())), preferred_element_type=F32)


def dot(a, b):
    return jnp.dot(a, b, preferred_element_type=F32)


def iota(shape, dim):
    return lax.broadcasted_iota(jnp.int32, shape, dim)


def panel_batches(side):
    def far(v):
        return min(v, side - v)

    offsets = [(dy, dz) for dy in range(side) for dz in range(side) if dy or dz]
    batches = [[], [], []]
    for dy, dz in offsets:
        if far(dy) == far(dz):
            batches[0].append((far(dy), dy, dz))
        elif far(dy) + far(dz) == 2:
            batches[1].append((0, dy, dz))
        else:
            batches[2].append((-far(dy) - far(dz), dy, dz))
    return [[dy * side + dz for _, dy, dz in sorted(batch)] for batch in batches]


def kernel(
    n_rep, n_tp, side,
    queries, new_kv, kv_cache, lengths, ids, owners, panels, weight,
    out,
    q_own, q_in, q_rows, o_rows, fresh, cache, w_buf, pool, pack_a, pack_b, pan_a, pan_b, spread, attn, attn_back, tags, place,
    far_y, hop_y, near_y, in_y, own_y, far_z, hop_z, near_z, in_z, own_z, fwd_a, got_a, fwd_b, got_b, base,
    tag_out, tag_in, disp, work, part, part_in, shrink, delta, delta_in,
    cache_sem, load_sem, pool_sem, q_send, q_recv, pa_send, pa_recv, pb_send, pb_recv, back_send, back_recv,
    hop_y_send, hop_y_recv, y_send, y_recv, hop_z_send, hop_z_recv, z_send, z_recv, a_send, a_recv, b_send, b_recv,
    tag_send, tag_recv, disp_send, disp_recv, part_send, part_recv, shr_send, shr_recv, del_send, del_recv,
):
    steps, rows, width = out.shape
    half = rows // 2
    heads = width // HD
    per_request = 2 * heads * steps
    total_rows = steps * rows
    part_width = width // 2
    bits = n_tp.bit_length() - 1
    cap_bits = CAP.bit_length() - 1

    rep = lax.axis_index("rep")
    t = lax.axis_index("tp")
    y, z = lax.div(t, side), lax.rem(t, side)
    member, group = lax.rem(t, 2), lax.div(t, 2)
    partner = t + 1 - 2 * member
    mine = pl.multiple_of(member * half, half)
    other = pl.multiple_of((1 - member) * half, half)

    def tp_peer(k):
        dy, dz = lax.div(k, side), lax.rem(k, side)
        return lax.rem(y + dy, side) * side + lax.rem(z + dz, side)

    chip, core = lax.div(rep, 2), lax.rem(rep, 2)
    chips = n_rep // 2

    def rep_peer(k):
        m, f = lax.div(k, 2), lax.rem(k, 2)
        return lax.rem(chip + m, chips) * 2 + lax.rem(core + f, 2)

    def remote(src, dst, send, recv, device):
        return pltpu.make_async_remote_copy(
            src_ref=src, dst_ref=dst, send_sem=send, recv_sem=recv, device_id=device, device_id_type=MESH
        )

    def landed(region, sem):
        pltpu.make_async_copy(region, region, sem.at[0]).wait()

    def over(low, high, body):
        def run(k, carry):
            body(k)
            return carry

        lax.fori_loop(low, high, run, 0)

    load_q = pltpu.make_async_copy(queries.at[:, pl.ds(mine, half), :], q_own, load_sem.at[0])
    load_fresh = pltpu.make_async_copy(
        new_kv.at[:, pl.ds(mine, half), pl.ds(pl.multiple_of(group * 2 * HD, 2 * HD), 2 * HD)], fresh, load_sem.at[1]
    )
    load_w = pltpu.make_async_copy(weight, w_buf, load_sem.at[2])

    def load_cache(c):
        span = pl.ds(c * KV_CHUNK, KV_CHUNK)
        return pltpu.make_async_copy(kv_cache.at[span], cache.at[span], cache_sem.at[c])

    def load_pool(p):
        span = pl.ds(pl.multiple_of(p * width, width), width)
        return pltpu.make_async_copy(panels.at[0, span, :], pool.at[p], pool_sem.at[p])

    barrier = pltpu.get_barrier_semaphore()
    for k in range(1, n_tp):
        pl.semaphore_signal(barrier, inc=1, device_id=(rep, tp_peer(k)), device_id_type=MESH)
    for k in range(1, n_rep):
        pl.semaphore_signal(barrier, inc=1, device_id=(rep_peer(k), t), device_id_type=MESH)
    over(0, n_tp, lambda p: load_pool(p).start())
    load_q.start()
    load_fresh.start()
    over(0, half // KV_CHUNK, lambda c: load_cache(c).start())
    half_width = width // 2
    low_half = iota((half_width, LANES), 1) < RANK

    def pack(p):
        load_pool(p).wait()
        top = pool[p, :half_width, :].astype(F32)
        bottom = pool[p, half_width:, :].astype(F32)
        pack_a[p] = jnp.where(low_half, top, pltpu.roll(bottom, RANK, 1)).astype(BF16)
        pack_b[p] = jnp.where(low_half, pltpu.roll(top, RANK, 1), bottom).astype(BF16)

    pan_cols = pl.ds(pl.multiple_of(t * LANES, LANES), LANES)

    def send_a(k):
        peer = tp_peer(k)
        return remote(pack_a.at[peer], pan_a.at[:, pan_cols], pa_send.at[0], pa_recv.at[0], (rep, peer))

    def send_b(k):
        peer = tp_peer(k)
        return remote(pack_b.at[peer], pan_b.at[:, pan_cols], pb_send.at[0], pb_recv.at[0], (rep, peer))

    pan_batches = panel_batches(side)
    spread_out = pan_batches[0] + pan_batches[1] + pan_batches[2]

    def start_all(send, batch):
        for k in pan_batches[batch]:
            send(k).start()

    over(0, n_tp, pack)

    pl.semaphore_wait(barrier, n_tp + n_rep - 2)

    def swap_q(part):
        span = pl.ds(pl.multiple_of(other + part * (half // 2), half // 2), half // 2)
        here = pl.ds(part * (half // 2), half // 2)
        return remote(queries.at[:, span, :], q_in.at[:, here, :], q_send.at[part], q_recv.at[part], (rep, partner))

    for part_of in range(2):
        swap_q(part_of).start()
    load_w.start()

    start_all(send_a, 0)
    start_all(send_a, 1)
    keep_a = pltpu.make_async_copy(pack_a.at[t], pan_a.at[:, pan_cols], load_sem.at[3])
    keep_b = pltpu.make_async_copy(pack_b.at[t], pan_b.at[:, pan_cols], load_sem.at[4])
    keep_a.start()
    keep_b.start()

    n_dest = n_rep * CAP
    n_adapters = owners.shape[1]
    diagonal = iota((rows, rows), 0) == iota((rows, rows), 1)
    earlier = jnp.where(iota((rows, rows), 1) < iota((rows, rows), 0), 1.0, 0.0).astype(BF16)
    dest = iota((rows, n_dest), 1)
    for s in range(steps):
        id_row = jnp.broadcast_to(ids[s : s + 1, :].astype(F32), (rows, rows))
        id_col = jnp.sum(jnp.where(diagonal, id_row, 0.0), axis=1, keepdims=True)
        found = iota((rows, n_adapters), 1).astype(F32) == id_col
        owner_row = jnp.broadcast_to(owners[...].astype(F32), (rows, n_adapters))
        slot = jnp.sum(jnp.where(found, owner_row, 0.0), axis=1, keepdims=True).astype(jnp.int32)
        holder = lax.shift_right_logical(slot, bits)
        goes = lax.shift_right_logical(dest, cap_bits) == holder
        rank = dot(earlier, jnp.where(goes, 1.0, 0.0).astype(BF16))
        here = goes & (rank == (dest & (CAP - 1)).astype(F32))
        place[s] = jnp.where(here, 1.0, 0.0).astype(BF16)
        tags[s] = jnp.where(iota((rows, LANES), 1) == (slot & (n_tp - 1)), 1.0, 0.0).astype(BF16)
    spread[...] = jnp.where(
        iota(spread.shape, 0) == lax.shift_right_logical(iota(spread.shape, 1), 7), 1.0, 0.0
    ).astype(BF16)

    for s in range(steps):
        sent = tn_dot(place[s], tags[s]).astype(BF16).reshape(n_rep, CAP, LANES)
        tag_out[:, s * CAP : (s + 1) * CAP, :] = sent

    def send_tag(k):
        peer = rep_peer(k)
        return remote(tag_out.at[peer], tag_in.at[rep], tag_send.at[0], tag_recv.at[0], (peer, t))

    for k in range(1, n_rep):
        send_tag(k).start()
    tag_in[rep] = tag_out[rep]

    load_q.wait()
    load_fresh.wait()
    for s in range(steps):
        for h in range(heads):
            cols = slice(h * HD, (h + 1) * HD)
            q_rows[pl.ds(h * steps + s, half, stride=per_request), :] = q_own[s, :, cols].astype(F32)

    scale = 1.0 / math.sqrt(HD)

    def rows_of(i):
        return pl.ds(pl.multiple_of(i * per_request, per_request), per_request)

    def attend_chunk(c):
        load_cache(c).wait()
        block = [c * KV_CHUNK + j for j in range(KV_CHUNK)]
        step_of = iota((per_request, 1), 0) & (steps - 1)
        fresh_rows = fresh[...].reshape(steps * half, 2 * HD)
        scores, own = [], []
        for i in block:
            q = q_rows[rows_of(i), :].astype(BF16)
            scores.append(nt_dot(q, cache[i, :, :HD]))
            own.append(nt_dot(q, fresh_rows[:, :HD]))
        total = []
        for j, i in enumerate(block):
            limit = jnp.zeros((per_request, 1), jnp.int32)
            for s in range(steps):
                limit = jnp.where(step_of == s, lengths[s, mine + i], limit)
            cached = jnp.where(iota(scores[j].shape, 1) < limit, scores[j] * scale, MASKED)
            fresh_score = jnp.where(iota(own[j].shape, 1) == step_of * half + i, own[j] * scale, MASKED)
            top = jnp.maximum(
                jnp.max(cached, axis=1, keepdims=True), jnp.max(fresh_score, axis=1, keepdims=True)
            )
            cached = jnp.exp(cached - top)
            fresh_score = jnp.exp(fresh_score - top)
            total.append(jnp.sum(cached, axis=1, keepdims=True) + jnp.sum(fresh_score, axis=1, keepdims=True))
            scores[j] = cached.astype(BF16)
            own[j] = fresh_score.astype(BF16)
        for j, i in enumerate(block):
            mixed = dot(scores[j], cache[i, :, HD:]) + dot(own[j], fresh_rows[:, HD:])
            o_rows[rows_of(i), :] = mixed / total[j]

    quarter = half // 2

    def swap_back(part):
        span = pl.ds(pl.multiple_of(mine + part * quarter, quarter), quarter)
        return remote(
            attn_back.at[:, pl.ds(part * quarter, quarter), :], attn.at[:, span, :],
            back_send.at[part], back_recv.at[part], (rep, partner),
        )

    for part_of in range(2):
        swap_q(part_of).wait()
        for s in range(steps):
            for h in range(heads):
                to = part_of * quarter * per_request + (heads + h) * steps + s
                arrived = q_in[s, part_of * quarter : (part_of + 1) * quarter, h * HD : (h + 1) * HD]
                q_rows[pl.ds(to, quarter, stride=per_request), :] = arrived.astype(F32)
        chunks = quarter // KV_CHUNK
        over(part_of * chunks, (part_of + 1) * chunks, attend_chunk)
        first = part_of * quarter * per_request
        span = pl.ds(pl.multiple_of(mine + part_of * quarter, quarter), quarter)
        back = slice(part_of * quarter, (part_of + 1) * quarter)
        for s in range(steps):
            for h in range(heads):
                cols = slice(h * HD, (h + 1) * HD)
                far_heads = o_rows[pl.ds(first + (heads + h) * steps + s, quarter, stride=per_request), :]
                attn_back[s, back, cols] = far_heads.astype(BF16)
        swap_back(part_of).start()
        for s in range(steps):
            for h in range(heads):
                cols = slice(h * HD, (h + 1) * HD)
                own_heads = o_rows[pl.ds(first + h * steps + s, quarter, stride=per_request), :]
                attn[s, span, cols] = own_heads.astype(BF16)
    start_all(send_a, 2)
    for part_of in range(2):
        swap_back(part_of).wait_recv()

    for s in range(steps):
        span = slice(s * CAP, (s + 1) * CAP)
        routed = tn_dot(place[s], attn[s]).astype(BF16)
        disp[:, span, :] = routed.reshape(n_rep, CAP, width)

    def send_disp(k):
        peer = rep_peer(k)
        return remote(disp.at[peer], work.at[rep], disp_send.at[0], disp_recv.at[k], (peer, t))

    near_first = (0, 1, chips - 1, 2)
    for m in near_first:
        for f in range(2):
            if m or f:
                send_disp(2 * m + f).start()
    work[rep] = disp[rep]

    load_w.wait()

    def project(block, part):
        cols = pl.ds(pl.multiple_of(block * width + part * part_width, part_width), part_width)
        return dot(attn[...].reshape(total_rows, width), w_buf[:, cols])

    half_total = total_rows // 2
    halves = (slice(0, half_total), slice(half_total, total_rows))

    def at_y(d):
        return lax.rem(y + d, side) * side + z

    def at_z(d):
        return y * side + lax.rem(z + d, side)

    def hop_along_y(way, j):
        return remote(
            far_y.at[way, j], hop_y.at[way, j], hop_y_send.at[0], hop_y_recv.at[way, j],
            (rep, at_y((side - 1, 1)[way])),
        )

    def hop_along_z(way, j):
        return remote(
            far_z.at[way, j], hop_z.at[way, j], hop_z_send.at[0], hop_z_recv.at[way, j],
            (rep, at_z((side - 1, 1)[way])),
        )

    def along_y(way, j):
        return remote(
            near_y.at[way, j], in_y.at[way, j], y_send.at[0], y_recv.at[way, j], (rep, at_y((side - 1, 1)[way]))
        )

    def along_z(way, j):
        return remote(
            near_z.at[way, j], in_z.at[way, j], z_send.at[0], z_recv.at[way, j], (rep, at_z((side - 1, 1)[way]))
        )

    def far_terms(j):
        to_z = lax.rem(z + 1 + j, side)
        to_y = lax.rem(y + 1 + j, side)
        term = project(lax.rem(y + 2, side) * side + to_z, 0).astype(BF16)
        for way in range(2):
            far_y[way, j] = term[halves[way]]
            hop_along_y(way, j).start()
        term = project(to_y * side + lax.rem(z + 2, side), 1).astype(BF16)
        for way in range(2):
            far_z[way, j] = term[halves[way]]
            hop_along_z(way, j).start()

    def near_terms(j):
        to_z = lax.rem(z + 1 + j, side)
        to_y = lax.rem(y + 1 + j, side)
        for way in range(2):
            d = (side - 1, 1)[way]
            term = project(lax.rem(y + d, side) * side + to_z, 0)
            near_y[way, j, halves[1 - way], :] = term[halves[1 - way]].astype(BF16)
            hop_along_y(way, j).wait_recv()
            near_y[way, j, halves[way], :] = (term[halves[way]] + hop_y[way, j].astype(F32)).astype(BF16)
            along_y(way, j).start()
            term = project(to_y * side + lax.rem(z + d, side), 1)
            near_z[way, j, halves[1 - way], :] = term[halves[1 - way]].astype(BF16)
            hop_along_z(way, j).wait_recv()
            near_z[way, j, halves[way], :] = (term[halves[way]] + hop_z[way, j].astype(F32)).astype(BF16)
            along_z(way, j).start()
        own_y[j] = project(y * side + to_z, 0)
        own_z[j] = project(to_y * side + z, 1)

    over(0, side, far_terms)
    start_all(send_b, 0)

    work_rows = n_rep * steps * CAP
    packed_rows = work_rows // 2
    tile = 2 * steps * CAP
    low_lanes = iota((tile, LANES), 1) < RANK
    low_all = (iota((tile, n_tp * LANES), 1) & (LANES - 1)) < RANK

    def masks(source):
        return dot(tag_in[pl.ds(2 * source, 2)].reshape(tile, LANES), spread[...])

    def packed(source):
        block = lax.rem(source, chips // 2)
        return pl.ds(pl.multiple_of(block * tile, tile), tile), source >= chips // 2

    landed(tag_in.at[pl.ds(0, n_rep - 1)], tag_recv)
    keep_a.wait()
    landed(pan_a.at[:, pl.ds(0, (n_tp - 1) * LANES)], pa_recv)
    for order, m in enumerate(near_first):
        for f in range(2):
            if m or f:
                send_disp(2 * m + f).wait_recv()
        source = lax.rem(chip + chips - m, chips)
        x = work[pl.ds(2 * source, 2)].reshape(tile, width)
        products = jnp.where(
            low_all, dot(x[:, :half_width], pan_a[...]), dot(x[:, half_width:], pan_a[...])
        ) * masks(source)
        total = products[:, :LANES]
        for a in range(1, n_tp):
            total = total + products[:, a * LANES : (a + 1) * LANES]
        total = total + pltpu.roll(total, RANK, 1)
        place_rows, upper = packed(source)
        if order < 2:
            part[place_rows, :] = total
        else:
            part[place_rows, :] = jnp.where(low_lanes != upper, total, part[place_rows, :])

    slab = packed_rows // n_tp

    def slab_of(device):
        return pl.ds(pl.multiple_of(device * slab, slab), slab)

    def send_part(k):
        peer = tp_peer(k)
        return remote(part.at[slab_of(peer)], part_in.at[k], part_send.at[0], part_recv.at[0], (rep, peer))

    for k in spread_out:
        send_part(k).start()
    start_all(send_b, 1)
    start_all(send_b, 2)

    def forward_y(j):
        device = (rep, y * side + lax.rem(z + 1 + j, side))
        return remote(fwd_a.at[j], got_a.at[j], a_send.at[0], a_recv.at[j], device)

    def forward_z(j):
        device = (rep, lax.rem(y + 1 + j, side) * side + z)
        return remote(fwd_b.at[j], got_b.at[j], b_send.at[0], b_recv.at[j], device)

    def gathered(own, arrived, copy, j):
        total = own[j]
        for way in range(2):
            copy(way, j).wait_recv()
            total = total + arrived[way, j].astype(F32)
        return total

    def second_stage(j):
        fwd_a[j] = gathered(own_y, in_y, along_y, j).astype(BF16)
        forward_y(j).start()
        fwd_b[j] = gathered(own_z, in_z, along_z, j).astype(BF16)
        forward_z(j).start()

    landed(part_in.at[pl.ds(1, n_tp - 1)], part_recv)
    total = part[slab_of(t), :]
    for k in range(1, n_tp):
        total = total + part_in[k]
    shrink[slab_of(t), :] = total.astype(BF16)

    def send_shrink(k):
        peer = tp_peer(k)
        return remote(shrink.at[slab_of(t)], shrink.at[slab_of(t)], shr_send.at[0], shr_recv.at[0], (rep, peer))

    for k in spread_out:
        send_shrink(k).start()
    over(0, side, near_terms)

    landed(shrink.at[pl.ds(0, (n_tp - 1) * slab)], shr_recv)

    keep_b.wait()
    landed(pan_b.at[:, pl.ds(0, (n_tp - 1) * LANES)], pb_recv)

    def send_delta(k):
        peer = rep_peer(k)
        return remote(delta.at[peer], delta_in.at[rep], del_send.at[0], del_recv.at[0], (peer, t))

    for m in near_first[::-1]:
        source = lax.rem(chip + m, chips)
        place_rows, upper = packed(source)
        shrunk = shrink[place_rows, :].astype(F32)
        turned = pltpu.roll(shrunk, RANK, 1)
        in_low = jnp.where(low_lanes, jnp.where(upper, turned, shrunk), 0.0)
        in_high = jnp.where(low_lanes, 0.0, jnp.where(upper, shrunk, turned))
        mask = masks(source)
        for side_of, placed in enumerate((in_low, in_high)):
            picked = (mask * jnp.concatenate([placed] * n_tp, axis=1)).astype(BF16)
            result = nt_dot(picked, pan_b[...]).astype(BF16)
            cols = slice(side_of * half_width, (side_of + 1) * half_width)
            delta[pl.ds(2 * source, 2), :, cols] = result.reshape(2, steps * CAP, half_width)
        for f in range(2):
            if m or f:
                send_delta(2 * m + f).start()
    delta_in[rep] = delta[rep]
    over(0, side - 1, second_stage)

    last = side - 1
    base[:, :part_width] = gathered(own_y, in_y, along_y, last)
    base[:, part_width:] = gathered(own_z, in_z, along_z, last)
    landed(delta_in.at[pl.ds(0, n_rep - 1)], del_recv)
    for s in range(steps):
        rows_in = delta_in[:, s * CAP : (s + 1) * CAP, :].reshape(n_dest, width)
        base[s * rows : (s + 1) * rows, :] += ADAPTER_SCALING * dot(place[s], rows_in)
    for j in range(last):
        forward_y(j).wait_recv()
        forward_z(j).wait_recv()
    for s in range(steps):
        span = slice(s * rows, (s + 1) * rows)
        for cols, got in ((slice(0, part_width), got_a), (slice(part_width, width), got_b)):
            total = base[span, cols]
            for j in range(last):
                total = total + got[j, span, :].astype(F32)
            out[s, :, cols] = total.astype(BF16)

    for part_of in range(2):
        swap_back(part_of).wait_send()
    landed(pack_a.at[pl.ds(0, n_tp - 1)], pa_send)
    landed(pack_b.at[pl.ds(0, n_tp - 1)], pb_send)
    landed(tag_out.at[pl.ds(0, n_rep - 1)], tag_send)
    landed(disp.at[pl.ds(0, n_rep - 1)], disp_send)
    landed(part_in.at[pl.ds(1, n_tp - 1)], part_send)
    landed(shrink.at[pl.ds(0, (n_tp - 1) * slab)], shr_send)
    landed(delta.at[pl.ds(0, n_rep - 1)], del_send)
    landed(far_y, hop_y_send)
    landed(far_z, hop_z_send)
    landed(near_y, y_send)
    landed(near_z, z_send)
    landed(fwd_a, a_send)
    landed(fwd_b, b_send)


def shards(n_rep, n_tp, queries, new_kv, kv_cache, lengths, adapter_ids, owner_slot, panels, out_weight):
    side = math.isqrt(n_tp)
    steps, rows, width = queries.shape
    half = rows // 2
    heads = width // HD
    total = steps * rows
    part = width // 2
    per_request = 2 * heads * steps
    work_rows = n_rep * steps * CAP
    dma = pltpu.SemaphoreType.DMA
    vmem = pltpu.VMEM
    hop = side - 1
    scratch = [
        vmem((steps, half, width), BF16),
        vmem((steps, half, width), BF16),
        vmem((half * per_request, HD), F32),
        vmem((half * per_request, HD), F32),
        vmem((steps, half, 2 * HD), BF16),
        vmem(kv_cache.shape, BF16),
        vmem(out_weight.shape, BF16),
        vmem((n_tp, width, LANES), BF16),
        vmem((n_tp, width // 2, LANES), BF16),
        vmem((n_tp, width // 2, LANES), BF16),
        vmem((width // 2, n_tp * LANES), BF16),
        vmem((width // 2, n_tp * LANES), BF16),
        vmem((LANES, n_tp * LANES), BF16),
        vmem((steps, rows, width), BF16),
        vmem((steps, half, width), BF16),
        vmem((steps, rows, LANES), BF16),
        vmem((steps, rows, n_rep * CAP), BF16),
        vmem((2, side, total // 2, part), BF16),
        vmem((2, side, total // 2, part), BF16),
        vmem((2, side, total, part), BF16),
        vmem((2, side, total, part), BF16),
        vmem((side, total, part), F32),
        vmem((2, side, total // 2, part), BF16),
        vmem((2, side, total // 2, part), BF16),
        vmem((2, side, total, part), BF16),
        vmem((2, side, total, part), BF16),
        vmem((side, total, part), F32),
        vmem((hop, total, part), BF16),
        vmem((hop, total, part), BF16),
        vmem((hop, total, part), BF16),
        vmem((hop, total, part), BF16),
        vmem((total, width), F32),
        vmem((n_rep, steps * CAP, LANES), BF16),
        vmem((n_rep, steps * CAP, LANES), BF16),
        vmem((n_rep, steps * CAP, width), BF16),
        vmem((n_rep, steps * CAP, width), BF16),
        vmem((work_rows // 2, LANES), F32),
        vmem((n_tp, work_rows // 2 // n_tp, LANES), F32),
        vmem((work_rows // 2, LANES), BF16),
        vmem((n_rep, steps * CAP, width), BF16),
        vmem((n_rep, steps * CAP, width), BF16),
        dma((half // KV_CHUNK,)),
        dma((5,)),
        dma((n_tp,)),
        dma((2,)), dma((2,)),
        dma((1,)), dma((1,)),
        dma((1,)), dma((1,)),
        dma((2,)), dma((2,)),
        dma((1,)), dma((2, side)),
        dma((1,)), dma((2, side)),
        dma((1,)), dma((2, side)),
        dma((1,)), dma((2, side)),
        dma((1,)), dma((hop,)),
        dma((1,)), dma((hop,)),
        dma((1,)), dma((1,)),
        dma((1,)), dma((n_rep,)),
        dma((1,)), dma((1,)),
        dma((1,)), dma((1,)),
        dma((1,)), dma((1,)),
    ]
    hbm = pl.BlockSpec(memory_space=pl.ANY)
    in_vmem = pl.BlockSpec(memory_space=pltpu.VMEM)
    in_smem = pl.BlockSpec(memory_space=pltpu.SMEM)
    return pl.pallas_call(
        functools.partial(kernel, n_rep, n_tp, side),
        out_shape=jax.ShapeDtypeStruct(queries.shape, BF16),
        in_specs=[hbm, hbm, hbm, in_smem, in_vmem, in_vmem, hbm, hbm],
        out_specs=in_vmem,
        scratch_shapes=scratch,
        compiler_params=pltpu.CompilerParams(
            collective_id=0, has_side_effects=True, vmem_limit_bytes=56 * 1024 * 1024
        ),
        cost_estimate=pl.CostEstimate(
            flops=5_000_000_000, bytes_accessed=20_000_000, transcendentals=600_000
        ),
    )(queries, new_kv, kv_cache, lengths, adapter_ids, owner_slot.reshape(1, -1), panels, out_weight)


def solution(mesh):
    placed = (
        P(None, "rep", "tp"),
        P(None, "rep", None),
        P("rep", None, "tp"),
        P(None, "rep"),
        P(None, "rep"),
        P(),
        P(("rep", "tp"), None, None),
        P("tp", None),
    )
    return jax.shard_map(
        functools.partial(shards, mesh.shape["rep"], mesh.shape["tp"]),
        mesh=mesh, in_specs=placed, out_specs=P(None, "rep", "tp"), check_vma=False,
    )
```

```python
import functools
import math

import jax
import jax.numpy as jnp
from jax import lax
from jax.experimental import pallas as pl
from jax.experimental.pallas import tpu as pltpu
from jax.sharding import PartitionSpec as P

MESH = pl.DeviceIdType.MESH
F32 = jnp.float32
BF16 = jnp.bfloat16

HD = 128
RANK = 64
CAP = 16
LANES = 128
KV_CHUNK = 8
ADAPTER_SCALING = 2.0
MASKED = -1e30


def nt_dot(a, b):
    return lax.dot_general(a, b, (((1,), (1,)), ((), ())), preferred_element_type=F32)


def tn_dot(a, b):
    return lax.dot_general(a, b, (((0,), (0,)), ((), ())), preferred_element_type=F32)


def dot(a, b):
    return jnp.dot(a, b, preferred_element_type=F32)


def iota(shape, dim):
    return lax.broadcasted_iota(jnp.int32, shape, dim)


def panel_batches(side):
    def far(v):
        return min(v, side - v)

    offsets = [(dy, dz) for dy in range(side) for dz in range(side) if dy or dz]
    batches = [[], [], []]
    for dy, dz in offsets:
        if far(dy) == far(dz):
            batches[0].append((far(dy), dy, dz))
        elif far(dy) + far(dz) == 2:
            batches[1].append((0, dy, dz))
        else:
            batches[2].append((-far(dy) - far(dz), dy, dz))
    return [[dy * side + dz for _, dy, dz in sorted(batch)] for batch in batches]


def kernel(
    n_rep, n_tp, side,
    queries, new_kv, kv_cache, lengths, ids, owners, panels, weight,
    out,
    q_own, q_in, q_rows, o_rows, fresh, cache, w_buf, pool, pack_a, pack_b, pan_a, pan_b, spread, attn, attn_back, tags, place,
    far_y, hop_y, near_y, in_y, own_y, far_z, hop_z, near_z, in_z, own_z, fwd_a, got_a, fwd_b, got_b, base,
    tag_out, tag_in, disp, work, part, part_in, shrink, delta, delta_in,
    cache_sem, load_sem, pool_sem, q_send, q_recv, pa_send, pa_recv, pb_send, pb_recv, back_send, back_recv,
    hop_y_send, hop_y_recv, y_send, y_recv, hop_z_send, hop_z_recv, z_send, z_recv, a_send, a_recv, b_send, b_recv,
    tag_send, tag_recv, disp_send, disp_recv, part_send, part_recv, shr_send, shr_recv, del_send, del_recv,
):
    steps, rows, width = out.shape
    half = rows // 2
    heads = width // HD
    per_request = 2 * heads * steps
    total_rows = steps * rows
    part_width = width // 2
    bits = n_tp.bit_length() - 1
    cap_bits = CAP.bit_length() - 1

    rep = lax.axis_index("rep")
    t = lax.axis_index("tp")
    y, z = lax.div(t, side), lax.rem(t, side)
    member, group = lax.rem(t, 2), lax.div(t, 2)
    partner = t + 1 - 2 * member
    mine = pl.multiple_of(member * half, half)
    other = pl.multiple_of((1 - member) * half, half)

    def tp_peer(k):
        dy, dz = lax.div(k, side), lax.rem(k, side)
        return lax.rem(y + dy, side) * side + lax.rem(z + dz, side)

    chip, core = lax.div(rep, 2), lax.rem(rep, 2)
    chips = n_rep // 2

    def rep_peer(k):
        m, f = lax.div(k, 2), lax.rem(k, 2)
        return lax.rem(chip + m, chips) * 2 + lax.rem(core + f, 2)

    def remote(src, dst, send, recv, device):
        return pltpu.make_async_remote_copy(
            src_ref=src, dst_ref=dst, send_sem=send, recv_sem=recv, device_id=device, device_id_type=MESH
        )

    def landed(region, sem):
        pltpu.make_async_copy(region, region, sem.at[0]).wait()

    def over(low, high, body):
        def run(k, carry):
            body(k)
            return carry

        lax.fori_loop(low, high, run, 0)

    load_q = pltpu.make_async_copy(queries.at[:, pl.ds(mine, half), :], q_own, load_sem.at[0])
    load_fresh = pltpu.make_async_copy(
        new_kv.at[:, pl.ds(mine, half), pl.ds(pl.multiple_of(group * 2 * HD, 2 * HD), 2 * HD)], fresh, load_sem.at[1]
    )
    load_w = pltpu.make_async_copy(weight, w_buf, load_sem.at[2])

    def load_cache(c):
        span = pl.ds(c * KV_CHUNK, KV_CHUNK)
        return pltpu.make_async_copy(kv_cache.at[span], cache.at[span], cache_sem.at[c])

    def load_pool(p):
        span = pl.ds(pl.multiple_of(p * width, width), width)
        return pltpu.make_async_copy(panels.at[0, span, :], pool.at[p], pool_sem.at[p])

    barrier = pltpu.get_barrier_semaphore()
    for k in sorted(range(1, n_tp), key=lambda k: -min(k // side, side - k // side) - min(k % side, side - k % side)):
        pl.semaphore_signal(barrier, inc=1, device_id=(rep, tp_peer(k)), device_id_type=MESH)
    for k in range(1, n_rep):
        pl.semaphore_signal(barrier, inc=1, device_id=(rep_peer(k), t), device_id_type=MESH)
    over(0, n_tp, lambda p: load_pool(p).start())
    load_q.start()
    load_fresh.start()
    over(0, half // KV_CHUNK, lambda c: load_cache(c).start())
    half_width = width // 2
    low_half = iota((half_width, LANES), 1) < RANK

    def pack(p):
        load_pool(p).wait()
        top = pool[p, :half_width, :].astype(F32)
        bottom = pool[p, half_width:, :].astype(F32)
        pack_a[p] = jnp.where(low_half, top, pltpu.roll(bottom, RANK, 1)).astype(BF16)
        pack_b[p] = jnp.where(low_half, pltpu.roll(top, RANK, 1), bottom).astype(BF16)

    pan_cols = pl.ds(pl.multiple_of(t * LANES, LANES), LANES)

    def send_a(k):
        peer = tp_peer(k)
        return remote(pack_a.at[peer], pan_a.at[:, pan_cols], pa_send.at[0], pa_recv.at[0], (rep, peer))

    def send_b(k):
        peer = tp_peer(k)
        return remote(pack_b.at[peer], pan_b.at[:, pan_cols], pb_send.at[0], pb_recv.at[0], (rep, peer))

    pan_batches = panel_batches(side)
    spread_out = pan_batches[0] + pan_batches[1] + pan_batches[2]

    def start_all(send, batch):
        for k in pan_batches[batch]:
            send(k).start()

    over(0, n_tp, pack)

    pl.semaphore_wait(barrier, n_tp + n_rep - 2)

    def swap_q(part):
        span = pl.ds(pl.multiple_of(other + part * (half // 2), half // 2), half // 2)
        here = pl.ds(part * (half // 2), half // 2)
        return remote(queries.at[:, span, :], q_in.at[:, here, :], q_send.at[part], q_recv.at[part], (rep, partner))

    for part_of in range(2):
        swap_q(part_of).start()
    load_w.start()

    start_all(send_a, 0)
    start_all(send_a, 1)
    keep_a = pltpu.make_async_copy(pack_a.at[t], pan_a.at[:, pan_cols], load_sem.at[3])
    keep_b = pltpu.make_async_copy(pack_b.at[t], pan_b.at[:, pan_cols], load_sem.at[4])
    keep_a.start()
    keep_b.start()

    load_q.wait()
    load_fresh.wait()
    for s in range(steps):
        for h in range(heads):
            cols = slice(h * HD, (h + 1) * HD)
            q_rows[pl.ds(h * steps + s, half, stride=per_request), :] = q_own[s, :, cols].astype(F32)

    scale = 1.0 / math.sqrt(HD)

    def rows_of(i):
        return pl.ds(pl.multiple_of(i * per_request, per_request), per_request)

    def attend_chunk(c):
        load_cache(c).wait()
        block = [c * KV_CHUNK + j for j in range(KV_CHUNK)]
        step_of = iota((per_request, 1), 0) & (steps - 1)
        fresh_rows = fresh[...].reshape(steps * half, 2 * HD)
        scores, own = [], []
        for i in block:
            q = q_rows[rows_of(i), :].astype(BF16)
            scores.append(nt_dot(q, cache[i, :, :HD]))
            own.append(nt_dot(q, fresh_rows[:, :HD]))
        total = []
        for j, i in enumerate(block):
            limit = jnp.zeros((per_request, 1), jnp.int32)
            for s in range(steps):
                limit = jnp.where(step_of == s, lengths[s, mine + i], limit)
            cached = jnp.where(iota(scores[j].shape, 1) < limit, scores[j] * scale, MASKED)
            fresh_score = jnp.where(iota(own[j].shape, 1) == step_of * half + i, own[j] * scale, MASKED)
            top = jnp.maximum(
                jnp.max(cached, axis=1, keepdims=True), jnp.max(fresh_score, axis=1, keepdims=True)
            )
            cached = jnp.exp(cached - top)
            fresh_score = jnp.exp(fresh_score - top)
            total.append(jnp.sum(cached, axis=1, keepdims=True) + jnp.sum(fresh_score, axis=1, keepdims=True))
            scores[j] = cached.astype(BF16)
            own[j] = fresh_score.astype(BF16)
        for j, i in enumerate(block):
            mixed = dot(scores[j], cache[i, :, HD:]) + dot(own[j], fresh_rows[:, HD:])
            o_rows[rows_of(i), :] = mixed / total[j]

    quarter = half // 2

    def swap_back(part):
        span = pl.ds(pl.multiple_of(mine + part * quarter, quarter), quarter)
        return remote(
            attn_back.at[:, pl.ds(part * quarter, quarter), :], attn.at[:, span, :],
            back_send.at[part], back_recv.at[part], (rep, partner),
        )

    for part_of in range(2):
        swap_q(part_of).wait()
        for s in range(steps):
            for h in range(heads):
                to = part_of * quarter * per_request + (heads + h) * steps + s
                arrived = q_in[s, part_of * quarter : (part_of + 1) * quarter, h * HD : (h + 1) * HD]
                q_rows[pl.ds(to, quarter, stride=per_request), :] = arrived.astype(F32)
        chunks = quarter // KV_CHUNK
        over(part_of * chunks, (part_of + 1) * chunks, attend_chunk)
        first = part_of * quarter * per_request
        back = slice(part_of * quarter, (part_of + 1) * quarter)
        for s in range(steps):
            for h in range(heads):
                cols = slice(h * HD, (h + 1) * HD)
                far_heads = o_rows[pl.ds(first + (heads + h) * steps + s, quarter, stride=per_request), :]
                attn_back[s, back, cols] = far_heads.astype(BF16)
        swap_back(part_of).start()
    for k in pan_batches[2][::-1]:
        send_a(k).start()
    for s in range(steps):
        for h in range(heads):
            cols = slice(h * HD, (h + 1) * HD)
            own_heads = o_rows[pl.ds(h * steps + s, half, stride=per_request), :]
            attn[s, pl.ds(mine, half), cols] = own_heads.astype(BF16)
    n_dest = n_rep * CAP
    n_adapters = owners.shape[1]
    diagonal = iota((rows, rows), 0) == iota((rows, rows), 1)
    earlier = jnp.where(iota((rows, rows), 1) < iota((rows, rows), 0), 1.0, 0.0).astype(BF16)
    dest = iota((rows, n_dest), 1)
    for s in range(steps):
        id_row = jnp.broadcast_to(ids[s : s + 1, :].astype(F32), (rows, rows))
        id_col = jnp.sum(jnp.where(diagonal, id_row, 0.0), axis=1, keepdims=True)
        found = iota((rows, n_adapters), 1).astype(F32) == id_col
        owner_row = jnp.broadcast_to(owners[...].astype(F32), (rows, n_adapters))
        slot = jnp.sum(jnp.where(found, owner_row, 0.0), axis=1, keepdims=True).astype(jnp.int32)
        holder = lax.shift_right_logical(slot, bits)
        goes = lax.shift_right_logical(dest, cap_bits) == holder
        rank = dot(earlier, jnp.where(goes, 1.0, 0.0).astype(BF16))
        here = goes & (rank == (dest & (CAP - 1)).astype(F32))
        place[s] = jnp.where(here, 1.0, 0.0).astype(BF16)
        tags[s] = jnp.where(iota((rows, LANES), 1) == (slot & (n_tp - 1)), 1.0, 0.0).astype(BF16)
    spread[...] = jnp.where(
        iota(spread.shape, 0) == lax.shift_right_logical(iota(spread.shape, 1), 7), 1.0, 0.0
    ).astype(BF16)

    for s in range(steps):
        sent = tn_dot(place[s], tags[s]).astype(BF16).reshape(n_rep, CAP, LANES)
        tag_out[:, s * CAP : (s + 1) * CAP, :] = sent

    def send_tag(k):
        peer = rep_peer(k)
        return remote(tag_out.at[peer], tag_in.at[rep], tag_send.at[0], tag_recv.at[0], (peer, t))

    for k in range(1, n_rep):
        send_tag(k).start()
    tag_in[rep] = tag_out[rep]

    for part_of in range(2):
        swap_back(part_of).wait_recv()

    for s in range(steps):
        span = slice(s * CAP, (s + 1) * CAP)
        routed = tn_dot(place[s], attn[s]).astype(BF16)
        disp[:, span, :] = routed.reshape(n_rep, CAP, width)

    def send_disp(k):
        peer = rep_peer(k)
        return remote(disp.at[peer], work.at[rep], disp_send.at[0], disp_recv.at[k], (peer, t))

    near_first = (0, 1, chips - 1, 2)
    for m in near_first:
        for f in range(2):
            if m or f:
                send_disp(2 * m + f).start()
    work[rep] = disp[rep]

    load_w.wait()

    def project(block, part):
        cols = pl.ds(pl.multiple_of(block * width + part * part_width, part_width), part_width)
        return dot(attn[...].reshape(total_rows, width), w_buf[:, cols])

    half_total = total_rows // 2
    halves = (slice(0, half_total), slice(half_total, total_rows))

    def at_y(d):
        return lax.rem(y + d, side) * side + z

    def at_z(d):
        return y * side + lax.rem(z + d, side)

    def hop_along_y(way, j):
        return remote(
            far_y.at[way, j], hop_y.at[way, j], hop_y_send.at[0], hop_y_recv.at[way, j],
            (rep, at_y((side - 1, 1)[way])),
        )

    def hop_along_z(way, j):
        return remote(
            far_z.at[way, j], hop_z.at[way, j], hop_z_send.at[0], hop_z_recv.at[way, j],
            (rep, at_z((side - 1, 1)[way])),
        )

    def along_y(way, j):
        return remote(
            near_y.at[way, j], in_y.at[way, j], y_send.at[0], y_recv.at[way, j], (rep, at_y((side - 1, 1)[way]))
        )

    def along_z(way, j):
        return remote(
            near_z.at[way, j], in_z.at[way, j], z_send.at[0], z_recv.at[way, j], (rep, at_z((side - 1, 1)[way]))
        )

    def far_terms(j):
        to_z = lax.rem(z + 1 + j, side)
        to_y = lax.rem(y + 1 + j, side)
        term = project(lax.rem(y + 2, side) * side + to_z, 0).astype(BF16)
        for way in range(2):
            far_y[way, j] = term[halves[way]]
            hop_along_y(way, j).start()
        term = project(to_y * side + lax.rem(z + 2, side), 1).astype(BF16)
        for way in range(2):
            far_z[way, j] = term[halves[way]]
            hop_along_z(way, j).start()

    def near_terms(j):
        to_z = lax.rem(z + 1 + j, side)
        to_y = lax.rem(y + 1 + j, side)
        for way in range(2):
            d = (side - 1, 1)[way]
            term = project(lax.rem(y + d, side) * side + to_z, 0)
            near_y[way, j, halves[1 - way], :] = term[halves[1 - way]].astype(BF16)
            hop_along_y(way, j).wait_recv()
            near_y[way, j, halves[way], :] = (term[halves[way]] + hop_y[way, j].astype(F32)).astype(BF16)
            along_y(way, j).start()
            term = project(to_y * side + lax.rem(z + d, side), 1)
            near_z[way, j, halves[1 - way], :] = term[halves[1 - way]].astype(BF16)
            hop_along_z(way, j).wait_recv()
            near_z[way, j, halves[way], :] = (term[halves[way]] + hop_z[way, j].astype(F32)).astype(BF16)
            along_z(way, j).start()
        own_y[j] = project(y * side + to_z, 0)
        own_z[j] = project(to_y * side + z, 1)

    over(0, side, far_terms)
    start_all(send_b, 0)

    work_rows = n_rep * steps * CAP
    packed_rows = work_rows // 2
    tile = 2 * steps * CAP
    low_lanes = iota((tile, LANES), 1) < RANK
    low_all = (iota((tile, n_tp * LANES), 1) & (LANES - 1)) < RANK

    def masks(source):
        return dot(tag_in[pl.ds(2 * source, 2)].reshape(tile, LANES), spread[...])

    def packed(source):
        block = lax.rem(source, chips // 2)
        return pl.ds(pl.multiple_of(block * tile, tile), tile), source >= chips // 2

    landed(tag_in.at[pl.ds(0, n_rep - 1)], tag_recv)
    keep_a.wait()
    landed(pan_a.at[:, pl.ds(0, (n_tp - 1) * LANES)], pa_recv)
    for order, m in enumerate(near_first):
        for f in range(2):
            if m or f:
                send_disp(2 * m + f).wait_recv()
        source = lax.rem(chip + chips - m, chips)
        x = work[pl.ds(2 * source, 2)].reshape(tile, width)
        products = jnp.where(
            low_all, dot(x[:, :half_width], pan_a[...]), dot(x[:, half_width:], pan_a[...])
        ) * masks(source)
        total = products[:, :LANES]
        for a in range(1, n_tp):
            total = total + products[:, a * LANES : (a + 1) * LANES]
        total = total + pltpu.roll(total, RANK, 1)
        place_rows, upper = packed(source)
        if order < 2:
            part[place_rows, :] = total
        else:
            part[place_rows, :] = jnp.where(low_lanes != upper, total, part[place_rows, :])

    slab = packed_rows // n_tp

    def slab_of(device):
        return pl.ds(pl.multiple_of(device * slab, slab), slab)

    def send_part(k):
        peer = tp_peer(k)
        return remote(part.at[slab_of(peer)], part_in.at[k], part_send.at[0], part_recv.at[0], (rep, peer))

    for k in spread_out:
        send_part(k).start()
    start_all(send_b, 1)
    start_all(send_b, 2)

    def forward_y(j):
        device = (rep, y * side + lax.rem(z + 1 + j, side))
        return remote(fwd_a.at[j], got_a.at[j], a_send.at[0], a_recv.at[j], device)

    def forward_z(j):
        device = (rep, lax.rem(y + 1 + j, side) * side + z)
        return remote(fwd_b.at[j], got_b.at[j], b_send.at[0], b_recv.at[j], device)

    def gathered(own, arrived, copy, j):
        total = own[j]
        for way in range(2):
            copy(way, j).wait_recv()
            total = total + arrived[way, j].astype(F32)
        return total

    def second_stage(j):
        fwd_a[j] = gathered(own_y, in_y, along_y, j).astype(BF16)
        forward_y(j).start()
        fwd_b[j] = gathered(own_z, in_z, along_z, j).astype(BF16)
        forward_z(j).start()

    landed(part_in.at[pl.ds(1, n_tp - 1)], part_recv)
    total = part[slab_of(t), :]
    for k in range(1, n_tp):
        total = total + part_in[k]
    shrink[slab_of(t), :] = total.astype(BF16)

    def send_shrink(k):
        peer = tp_peer(k)
        return remote(shrink.at[slab_of(t)], shrink.at[slab_of(t)], shr_send.at[0], shr_recv.at[0], (rep, peer))

    for k in spread_out:
        send_shrink(k).start()
    over(0, side, near_terms)

    landed(shrink.at[pl.ds(0, (n_tp - 1) * slab)], shr_recv)

    keep_b.wait()
    landed(pan_b.at[:, pl.ds(0, (n_tp - 1) * LANES)], pb_recv)

    def send_delta(k):
        peer = rep_peer(k)
        return remote(delta.at[peer], delta_in.at[rep], del_send.at[0], del_recv.at[0], (peer, t))

    for m in near_first[::-1]:
        source = lax.rem(chip + m, chips)
        place_rows, upper = packed(source)
        shrunk = shrink[place_rows, :].astype(F32)
        turned = pltpu.roll(shrunk, RANK, 1)
        in_low = jnp.where(low_lanes, jnp.where(upper, turned, shrunk), 0.0)
        in_high = jnp.where(low_lanes, 0.0, jnp.where(upper, shrunk, turned))
        mask = masks(source)
        for side_of, placed in enumerate((in_low, in_high)):
            picked = (mask * jnp.concatenate([placed] * n_tp, axis=1)).astype(BF16)
            result = nt_dot(picked, pan_b[...]).astype(BF16)
            cols = slice(side_of * half_width, (side_of + 1) * half_width)
            delta[pl.ds(2 * source, 2), :, cols] = result.reshape(2, steps * CAP, half_width)
        for f in range(2):
            if m or f:
                send_delta(2 * m + f).start()
    delta_in[rep] = delta[rep]
    over(0, side - 1, second_stage)

    last = side - 1
    base[:, :part_width] = gathered(own_y, in_y, along_y, last)
    base[:, part_width:] = gathered(own_z, in_z, along_z, last)
    landed(delta_in.at[pl.ds(0, n_rep - 1)], del_recv)
    for s in range(steps):
        rows_in = delta_in[:, s * CAP : (s + 1) * CAP, :].reshape(n_dest, width)
        base[s * rows : (s + 1) * rows, :] += ADAPTER_SCALING * dot(place[s], rows_in)
    for j in range(last):
        forward_y(j).wait_recv()
        forward_z(j).wait_recv()
    for s in range(steps):
        span = slice(s * rows, (s + 1) * rows)
        for cols, got in ((slice(0, part_width), got_a), (slice(part_width, width), got_b)):
            total = base[span, cols]
            for j in range(last):
                total = total + got[j, span, :].astype(F32)
            out[s, :, cols] = total.astype(BF16)

    for part_of in range(2):
        swap_back(part_of).wait_send()
    landed(pack_a.at[pl.ds(0, n_tp - 1)], pa_send)
    landed(pack_b.at[pl.ds(0, n_tp - 1)], pb_send)
    landed(tag_out.at[pl.ds(0, n_rep - 1)], tag_send)
    landed(disp.at[pl.ds(0, n_rep - 1)], disp_send)
    landed(part_in.at[pl.ds(1, n_tp - 1)], part_send)
    landed(shrink.at[pl.ds(0, (n_tp - 1) * slab)], shr_send)
    landed(delta.at[pl.ds(0, n_rep - 1)], del_send)
    landed(far_y, hop_y_send)
    landed(far_z, hop_z_send)
    landed(near_y, y_send)
    landed(near_z, z_send)
    landed(fwd_a, a_send)
    landed(fwd_b, b_send)


def shards(n_rep, n_tp, queries, new_kv, kv_cache, lengths, adapter_ids, owner_slot, panels, out_weight):
    side = math.isqrt(n_tp)
    steps, rows, width = queries.shape
    half = rows // 2
    heads = width // HD
    total = steps * rows
    part = width // 2
    per_request = 2 * heads * steps
    work_rows = n_rep * steps * CAP
    dma = pltpu.SemaphoreType.DMA
    vmem = pltpu.VMEM
    hop = side - 1
    scratch = [
        vmem((steps, half, width), BF16),
        vmem((steps, half, width), BF16),
        vmem((half * per_request, HD), F32),
        vmem((half * per_request, HD), F32),
        vmem((steps, half, 2 * HD), BF16),
        vmem(kv_cache.shape, BF16),
        vmem(out_weight.shape, BF16),
        vmem((n_tp, width, LANES), BF16),
        vmem((n_tp, width // 2, LANES), BF16),
        vmem((n_tp, width // 2, LANES), BF16),
        vmem((width // 2, n_tp * LANES), BF16),
        vmem((width // 2, n_tp * LANES), BF16),
        vmem((LANES, n_tp * LANES), BF16),
        vmem((steps, rows, width), BF16),
        vmem((steps, half, width), BF16),
        vmem((steps, rows, LANES), BF16),
        vmem((steps, rows, n_rep * CAP), BF16),
        vmem((2, side, total // 2, part), BF16),
        vmem((2, side, total // 2, part), BF16),
        vmem((2, side, total, part), BF16),
        vmem((2, side, total, part), BF16),
        vmem((side, total, part), F32),
        vmem((2, side, total // 2, part), BF16),
        vmem((2, side, total // 2, part), BF16),
        vmem((2, side, total, part), BF16),
        vmem((2, side, total, part), BF16),
        vmem((side, total, part), F32),
        vmem((hop, total, part), BF16),
        vmem((hop, total, part), BF16),
        vmem((hop, total, part), BF16),
        vmem((hop, total, part), BF16),
        vmem((total, width), F32),
        vmem((n_rep, steps * CAP, LANES), BF16),
        vmem((n_rep, steps * CAP, LANES), BF16),
        vmem((n_rep, steps * CAP, width), BF16),
        vmem((n_rep, steps * CAP, width), BF16),
        vmem((work_rows // 2, LANES), F32),
        vmem((n_tp, work_rows // 2 // n_tp, LANES), F32),
        vmem((work_rows // 2, LANES), BF16),
        vmem((n_rep, steps * CAP, width), BF16),
        vmem((n_rep, steps * CAP, width), BF16),
        dma((half // KV_CHUNK,)),
        dma((5,)),
        dma((n_tp,)),
        dma((2,)), dma((2,)),
        dma((1,)), dma((1,)),
        dma((1,)), dma((1,)),
        dma((2,)), dma((2,)),
        dma((1,)), dma((2, side)),
        dma((1,)), dma((2, side)),
        dma((1,)), dma((2, side)),
        dma((1,)), dma((2, side)),
        dma((1,)), dma((hop,)),
        dma((1,)), dma((hop,)),
        dma((1,)), dma((1,)),
        dma((1,)), dma((n_rep,)),
        dma((1,)), dma((1,)),
        dma((1,)), dma((1,)),
        dma((1,)), dma((1,)),
    ]
    hbm = pl.BlockSpec(memory_space=pl.ANY)
    in_vmem = pl.BlockSpec(memory_space=pltpu.VMEM)
    in_smem = pl.BlockSpec(memory_space=pltpu.SMEM)
    return pl.pallas_call(
        functools.partial(kernel, n_rep, n_tp, side),
        out_shape=jax.ShapeDtypeStruct(queries.shape, BF16),
        in_specs=[hbm, hbm, hbm, in_smem, in_vmem, in_vmem, hbm, hbm],
        out_specs=in_vmem,
        scratch_shapes=scratch,
        compiler_params=pltpu.CompilerParams(
            collective_id=0, has_side_effects=True, vmem_limit_bytes=56 * 1024 * 1024
        ),
        cost_estimate=pl.CostEstimate(
            flops=5_000_000_000, bytes_accessed=20_000_000, transcendentals=600_000
        ),
    )(queries, new_kv, kv_cache, lengths, adapter_ids, owner_slot.reshape(1, -1), panels, out_weight)


def solution(mesh):
    placed = (
        P(None, "rep", "tp"),
        P(None, "rep", None),
        P("rep", None, "tp"),
        P(None, "rep"),
        P(None, "rep"),
        P(),
        P(("rep", "tp"), None, None),
        P("tp", None),
    )
    return jax.shard_map(
        functools.partial(shards, mesh.shape["rep"], mesh.shape["tp"]),
        mesh=mesh, in_specs=placed, out_specs=P(None, "rep", "tp"), check_vma=False,
    )
```

```python
import functools
import math

import jax
import jax.numpy as jnp
from jax import lax
from jax.experimental import pallas as pl
from jax.experimental.pallas import tpu as pltpu
from jax.sharding import PartitionSpec as P

MESH = pl.DeviceIdType.MESH
F32 = jnp.float32
BF16 = jnp.bfloat16

HD = 128
RANK = 64
CAP = 16
LANES = 128
KV_CHUNK = 8
ADAPTER_SCALING = 2.0
MASKED = -1e30


def nt_dot(a, b):
    return lax.dot_general(a, b, (((1,), (1,)), ((), ())), preferred_element_type=F32)


def tn_dot(a, b):
    return lax.dot_general(a, b, (((0,), (0,)), ((), ())), preferred_element_type=F32)


def dot(a, b):
    return jnp.dot(a, b, preferred_element_type=F32)


def iota(shape, dim):
    return lax.broadcasted_iota(jnp.int32, shape, dim)


def panel_batches(side):
    def far(v):
        return min(v, side - v)

    offsets = [(dy, dz) for dy in range(side) for dz in range(side) if dy or dz]
    batches = [[], [], []]
    for dy, dz in offsets:
        if far(dy) == far(dz):
            batches[0].append((far(dy), dy, dz))
        elif far(dy) + far(dz) == 2:
            batches[1].append((0, dy, dz))
        else:
            batches[2].append((-far(dy) - far(dz), dy, dz))
    return [[dy * side + dz for _, dy, dz in sorted(batch)] for batch in batches]


def kernel(
    n_rep, n_tp, side,
    queries, new_kv, kv_cache, lengths, ids, owners, panels, weight,
    out,
    q_own, q_in, q_rows, o_rows, fresh, cache, w_buf, pool, pack_a, pack_b, pan_a, pan_b, spread, attn, attn_back, tags, place,
    far_y, hop_y, near_y, in_y, own_y, far_z, hop_z, near_z, in_z, own_z, fwd_a, got_a, fwd_b, got_b, base,
    tag_out, tag_in, disp, work, part, part_in, shrink, delta, delta_in,
    cache_sem, load_sem, pool_sem, q_send, q_recv, pa_send, pa_recv, pb_send, pb_recv, back_send, back_recv,
    hop_y_send, hop_y_recv, y_send, y_recv, hop_z_send, hop_z_recv, z_send, z_recv, a_send, a_recv, b_send, b_recv,
    tag_send, tag_recv, disp_send, disp_recv, part_send, part_recv, shr_send, shr_recv, del_send, del_recv,
):
    steps, rows, width = out.shape
    half = rows // 2
    heads = width // HD
    per_request = 2 * heads * steps
    total_rows = steps * rows
    part_width = width // 2
    bits = n_tp.bit_length() - 1
    cap_bits = CAP.bit_length() - 1

    rep = lax.axis_index("rep")
    t = lax.axis_index("tp")
    y, z = lax.div(t, side), lax.rem(t, side)
    member, group = lax.rem(t, 2), lax.div(t, 2)
    partner = t + 1 - 2 * member
    mine = pl.multiple_of(member * half, half)
    other = pl.multiple_of((1 - member) * half, half)

    def tp_peer(k):
        dy, dz = lax.div(k, side), lax.rem(k, side)
        return lax.rem(y + dy, side) * side + lax.rem(z + dz, side)

    chip, core = lax.div(rep, 2), lax.rem(rep, 2)
    chips = n_rep // 2

    def rep_peer(k):
        m, f = lax.div(k, 2), lax.rem(k, 2)
        return lax.rem(chip + m, chips) * 2 + lax.rem(core + f, 2)

    def remote(src, dst, send, recv, device):
        return pltpu.make_async_remote_copy(
            src_ref=src, dst_ref=dst, send_sem=send, recv_sem=recv, device_id=device, device_id_type=MESH
        )

    def landed(region, sem):
        pltpu.make_async_copy(region, region, sem.at[0]).wait()

    def over(low, high, body):
        def run(k, carry):
            body(k)
            return carry

        lax.fori_loop(low, high, run, 0)

    load_q = pltpu.make_async_copy(queries.at[:, pl.ds(mine, half), :], q_own, load_sem.at[0])
    load_fresh = pltpu.make_async_copy(
        new_kv.at[:, pl.ds(mine, half), pl.ds(pl.multiple_of(group * 2 * HD, 2 * HD), 2 * HD)], fresh, load_sem.at[1]
    )
    load_w = pltpu.make_async_copy(weight, w_buf, load_sem.at[2])

    def load_cache(c):
        span = pl.ds(c * KV_CHUNK, KV_CHUNK)
        return pltpu.make_async_copy(kv_cache.at[span], cache.at[span], cache_sem.at[c])

    def load_pool(p):
        span = pl.ds(pl.multiple_of(p * width, width), width)
        return pltpu.make_async_copy(panels.at[0, span, :], pool.at[p], pool_sem.at[p])

    barrier = pltpu.get_barrier_semaphore()
    for k in sorted(range(1, n_tp), key=lambda k: -min(k // side, side - k // side) - min(k % side, side - k % side)):
        pl.semaphore_signal(barrier, inc=1, device_id=(rep, tp_peer(k)), device_id_type=MESH)
    for k in range(1, n_rep):
        pl.semaphore_signal(barrier, inc=1, device_id=(rep_peer(k), t), device_id_type=MESH)
    over(0, n_tp, lambda p: load_pool(p).start())
    load_q.start()
    load_fresh.start()
    over(0, half // KV_CHUNK, lambda c: load_cache(c).start())
    half_width = width // 2
    low_half = iota((half_width, LANES), 1) < RANK

    def pack(p):
        load_pool(p).wait()
        top = pool[p, :half_width, :].astype(F32)
        bottom = pool[p, half_width:, :].astype(F32)
        pack_a[p] = jnp.where(low_half, top, pltpu.roll(bottom, RANK, 1)).astype(BF16)
        pack_b[p] = jnp.where(low_half, pltpu.roll(top, RANK, 1), bottom).astype(BF16)

    pan_cols = pl.ds(pl.multiple_of(t * LANES, LANES), LANES)

    def send_a(k):
        peer = tp_peer(k)
        return remote(pack_a.at[peer], pan_a.at[:, pan_cols], pa_send.at[0], pa_recv.at[0], (rep, peer))

    def send_b(k):
        peer = tp_peer(k)
        return remote(pack_b.at[peer], pan_b.at[:, pan_cols], pb_send.at[0], pb_recv.at[0], (rep, peer))

    pan_batches = panel_batches(side)
    spread_out = pan_batches[0] + pan_batches[1] + pan_batches[2]

    def start_all(send, batch):
        for k in pan_batches[batch]:
            send(k).start()

    over(0, n_tp, pack)

    pl.semaphore_wait(barrier, n_tp + n_rep - 2)

    def swap_q(part):
        span = pl.ds(pl.multiple_of(other + part * (half // 2), half // 2), half // 2)
        here = pl.ds(part * (half // 2), half // 2)
        return remote(queries.at[:, span, :], q_in.at[:, here, :], q_send.at[part], q_recv.at[part], (rep, partner))

    for part_of in range(2):
        swap_q(part_of).start()
    load_w.start()

    start_all(send_a, 0)
    start_all(send_a, 1)
    keep_a = pltpu.make_async_copy(pack_a.at[t], pan_a.at[:, pan_cols], load_sem.at[3])
    keep_b = pltpu.make_async_copy(pack_b.at[t], pan_b.at[:, pan_cols], load_sem.at[4])
    keep_a.start()
    keep_b.start()

    load_q.wait()
    load_fresh.wait()
    for s in range(steps):
        for h in range(heads):
            cols = slice(h * HD, (h + 1) * HD)
            q_rows[pl.ds(h * steps + s, half, stride=per_request), :] = q_own[s, :, cols].astype(F32)

    scale = 1.0 / math.sqrt(HD)

    def rows_of(i):
        return pl.ds(pl.multiple_of(i * per_request, per_request), per_request)

    def attend_chunk(c):
        load_cache(c).wait()
        block = [c * KV_CHUNK + j for j in range(KV_CHUNK)]
        step_of = iota((per_request, 1), 0) & (steps - 1)
        fresh_rows = fresh[...].reshape(steps * half, 2 * HD)
        scores, own = [], []
        for i in block:
            q = q_rows[rows_of(i), :].astype(BF16)
            scores.append(nt_dot(q, cache[i, :, :HD]))
            own.append(nt_dot(q, fresh_rows[:, :HD]))
        total = []
        for j, i in enumerate(block):
            limit = jnp.zeros((per_request, 1), jnp.int32)
            for s in range(steps):
                limit = jnp.where(step_of == s, lengths[s, mine + i], limit)
            cached = jnp.where(iota(scores[j].shape, 1) < limit, scores[j] * scale, MASKED)
            fresh_score = jnp.where(iota(own[j].shape, 1) == step_of * half + i, own[j] * scale, MASKED)
            top = jnp.maximum(
                jnp.max(cached, axis=1, keepdims=True), jnp.max(fresh_score, axis=1, keepdims=True)
            )
            cached = jnp.exp(cached - top)
            fresh_score = jnp.exp(fresh_score - top)
            total.append(jnp.sum(cached, axis=1, keepdims=True) + jnp.sum(fresh_score, axis=1, keepdims=True))
            scores[j] = cached.astype(BF16)
            own[j] = fresh_score.astype(BF16)
        for j, i in enumerate(block):
            mixed = dot(scores[j], cache[i, :, HD:]) + dot(own[j], fresh_rows[:, HD:])
            o_rows[rows_of(i), :] = mixed / total[j]

    quarter = half // 2

    def swap_back(part):
        span = pl.ds(pl.multiple_of(mine + part * quarter, quarter), quarter)
        return remote(
            attn_back.at[:, pl.ds(part * quarter, quarter), :], attn.at[:, span, :],
            back_send.at[part], back_recv.at[part], (rep, partner),
        )

    for part_of in range(2):
        swap_q(part_of).wait()
        for s in range(steps):
            for h in range(heads):
                to = part_of * quarter * per_request + (heads + h) * steps + s
                arrived = q_in[s, part_of * quarter : (part_of + 1) * quarter, h * HD : (h + 1) * HD]
                q_rows[pl.ds(to, quarter, stride=per_request), :] = arrived.astype(F32)
        chunks = quarter // KV_CHUNK
        over(part_of * chunks, (part_of + 1) * chunks, attend_chunk)
        first = part_of * quarter * per_request
        back = slice(part_of * quarter, (part_of + 1) * quarter)
        for s in range(steps):
            for h in range(heads):
                cols = slice(h * HD, (h + 1) * HD)
                far_heads = o_rows[pl.ds(first + (heads + h) * steps + s, quarter, stride=per_request), :]
                attn_back[s, back, cols] = far_heads.astype(BF16)
        swap_back(part_of).start()
    for k in pan_batches[2][::-1]:
        send_a(k).start()
    for s in range(steps):
        for h in range(heads):
            cols = slice(h * HD, (h + 1) * HD)
            own_heads = o_rows[pl.ds(h * steps + s, half, stride=per_request), :]
            attn[s, pl.ds(mine, half), cols] = own_heads.astype(BF16)
    n_dest = n_rep * CAP
    n_adapters = owners.shape[1]
    diagonal = iota((rows, rows), 0) == iota((rows, rows), 1)
    earlier = jnp.where(iota((rows, rows), 1) < iota((rows, rows), 0), 1.0, 0.0).astype(BF16)
    dest = iota((rows, n_dest), 1)
    for s in range(steps):
        id_row = jnp.broadcast_to(ids[s : s + 1, :].astype(F32), (rows, rows))
        id_col = jnp.sum(jnp.where(diagonal, id_row, 0.0), axis=1, keepdims=True)
        found = iota((rows, n_adapters), 1).astype(F32) == id_col
        owner_row = jnp.broadcast_to(owners[...].astype(F32), (rows, n_adapters))
        slot = jnp.sum(jnp.where(found, owner_row, 0.0), axis=1, keepdims=True).astype(jnp.int32)
        holder = lax.shift_right_logical(slot, bits)
        goes = lax.shift_right_logical(dest, cap_bits) == holder
        rank = dot(earlier, jnp.where(goes, 1.0, 0.0).astype(BF16))
        here = goes & (rank == (dest & (CAP - 1)).astype(F32))
        place[s] = jnp.where(here, 1.0, 0.0).astype(BF16)
        tags[s] = jnp.where(iota((rows, LANES), 1) == (slot & (n_tp - 1)), 1.0, 0.0).astype(BF16)
    spread[...] = jnp.where(
        iota(spread.shape, 0) == lax.shift_right_logical(iota(spread.shape, 1), 7), 1.0, 0.0
    ).astype(BF16)

    for s in range(steps):
        sent = tn_dot(place[s], tags[s]).astype(BF16).reshape(n_rep, CAP, LANES)
        tag_out[:, s * CAP : (s + 1) * CAP, :] = sent

    def send_tag(k):
        peer = rep_peer(k)
        return remote(tag_out.at[peer], tag_in.at[rep], tag_send.at[0], tag_recv.at[0], (peer, t))

    for k in range(1, n_rep):
        send_tag(k).start()
    tag_in[rep] = tag_out[rep]

    for part_of in range(2):
        swap_back(part_of).wait_recv()

    for s in range(steps):
        span = slice(s * CAP, (s + 1) * CAP)
        routed = tn_dot(place[s], attn[s]).astype(BF16)
        disp[:, span, :] = routed.reshape(n_rep, CAP, width)

    def send_disp(k):
        peer = rep_peer(k)
        return remote(disp.at[peer], work.at[rep], disp_send.at[0], disp_recv.at[k], (peer, t))

    near_first = (0, 1, chips - 1, 2)
    for m in near_first:
        for f in range(2):
            if m or f:
                send_disp(2 * m + f).start()
    work[rep] = disp[rep]

    load_w.wait()

    def project(block, part):
        cols = pl.ds(pl.multiple_of(block * width + part * part_width, part_width), part_width)
        return dot(attn[...].reshape(total_rows, width), w_buf[:, cols])

    half_total = total_rows // 2
    halves = (slice(0, half_total), slice(half_total, total_rows))

    def at_y(d):
        return lax.rem(y + d, side) * side + z

    def at_z(d):
        return y * side + lax.rem(z + d, side)

    def hop_along_y(way, j):
        return remote(
            far_y.at[way, j], hop_y.at[way, j], hop_y_send.at[0], hop_y_recv.at[way, j],
            (rep, at_y((side - 1, 1)[way])),
        )

    def hop_along_z(way, j):
        return remote(
            far_z.at[way, j], hop_z.at[way, j], hop_z_send.at[0], hop_z_recv.at[way, j],
            (rep, at_z((side - 1, 1)[way])),
        )

    def along_y(way, j):
        return remote(
            near_y.at[way, j], in_y.at[way, j], y_send.at[0], y_recv.at[way, j], (rep, at_y((side - 1, 1)[way]))
        )

    def along_z(way, j):
        return remote(
            near_z.at[way, j], in_z.at[way, j], z_send.at[0], z_recv.at[way, j], (rep, at_z((side - 1, 1)[way]))
        )

    def far_terms(j):
        to_z = lax.rem(z + 1 + j, side)
        to_y = lax.rem(y + 1 + j, side)
        term = project(lax.rem(y + 2, side) * side + to_z, 0).astype(BF16)
        for way in range(2):
            far_y[way, j] = term[halves[way]]
            hop_along_y(way, j).start()
        term = project(to_y * side + lax.rem(z + 2, side), 1).astype(BF16)
        for way in range(2):
            far_z[way, j] = term[halves[way]]
            hop_along_z(way, j).start()

    def near_terms(j):
        to_z = lax.rem(z + 1 + j, side)
        to_y = lax.rem(y + 1 + j, side)
        for way in range(2):
            d = (side - 1, 1)[way]
            term = project(lax.rem(y + d, side) * side + to_z, 0)
            near_y[way, j, halves[1 - way], :] = term[halves[1 - way]].astype(BF16)
            hop_along_y(way, j).wait_recv()
            near_y[way, j, halves[way], :] = (term[halves[way]] + hop_y[way, j].astype(F32)).astype(BF16)
            along_y(way, j).start()
            term = project(to_y * side + lax.rem(z + d, side), 1)
            near_z[way, j, halves[1 - way], :] = term[halves[1 - way]].astype(BF16)
            hop_along_z(way, j).wait_recv()
            near_z[way, j, halves[way], :] = (term[halves[way]] + hop_z[way, j].astype(F32)).astype(BF16)
            along_z(way, j).start()
        own_y[j] = project(y * side + to_z, 0)
        own_z[j] = project(to_y * side + z, 1)

    over(0, side, far_terms)
    start_all(send_b, 0)

    work_rows = n_rep * steps * CAP
    packed_rows = work_rows // 2
    tile = 2 * steps * CAP
    low_lanes = iota((tile, LANES), 1) < RANK
    low_all = (iota((tile, n_tp * LANES), 1) & (LANES - 1)) < RANK

    def masks(source):
        return dot(tag_in[pl.ds(2 * source, 2)].reshape(tile, LANES), spread[...])

    def packed(source):
        block = lax.rem(source, chips // 2)
        return pl.ds(pl.multiple_of(block * tile, tile), tile), source >= chips // 2

    landed(tag_in.at[pl.ds(0, n_rep - 1)], tag_recv)
    keep_a.wait()
    landed(pan_a.at[:, pl.ds(0, (n_tp - 1) * LANES)], pa_recv)
    for order, m in enumerate(near_first):
        for f in range(2):
            if m or f:
                send_disp(2 * m + f).wait_recv()
        source = lax.rem(chip + chips - m, chips)
        x = work[pl.ds(2 * source, 2)].reshape(tile, width)
        products = jnp.where(
            low_all, dot(x[:, :half_width], pan_a[...]), dot(x[:, half_width:], pan_a[...])
        ) * masks(source)
        total = products[:, :LANES]
        for a in range(1, n_tp):
            total = total + products[:, a * LANES : (a + 1) * LANES]
        total = total + pltpu.roll(total, RANK, 1)
        place_rows, upper = packed(source)
        if order < 2:
            part[place_rows, :] = total
        else:
            part[place_rows, :] = jnp.where(low_lanes != upper, total, part[place_rows, :])

    slab = packed_rows // n_tp

    def slab_of(device):
        return pl.ds(pl.multiple_of(device * slab, slab), slab)

    def send_part(k):
        peer = tp_peer(k)
        return remote(part.at[slab_of(peer)], part_in.at[k], part_send.at[0], part_recv.at[0], (rep, peer))

    for k in spread_out:
        send_part(k).start()
    start_all(send_b, 1)
    for k in pan_batches[2][::-1]:
        send_b(k).start()

    def forward_y(j):
        device = (rep, y * side + lax.rem(z + 1 + j, side))
        return remote(fwd_a.at[j], got_a.at[j], a_send.at[0], a_recv.at[j], device)

    def forward_z(j):
        device = (rep, lax.rem(y + 1 + j, side) * side + z)
        return remote(fwd_b.at[j], got_b.at[j], b_send.at[0], b_recv.at[j], device)

    def gathered(own, arrived, copy, j):
        total = own[j]
        for way in range(2):
            copy(way, j).wait_recv()
            total = total + arrived[way, j].astype(F32)
        return total

    def second_stage(j):
        fwd_a[j] = gathered(own_y, in_y, along_y, j).astype(BF16)
        forward_y(j).start()
        fwd_b[j] = gathered(own_z, in_z, along_z, j).astype(BF16)
        forward_z(j).start()

    landed(part_in.at[pl.ds(1, n_tp - 1)], part_recv)
    total = part[slab_of(t), :]
    for k in range(1, n_tp):
        total = total + part_in[k]
    shrink[slab_of(t), :] = total.astype(BF16)

    def send_shrink(k):
        peer = tp_peer(k)
        return remote(shrink.at[slab_of(t)], shrink.at[slab_of(t)], shr_send.at[0], shr_recv.at[0], (rep, peer))

    for k in spread_out:
        send_shrink(k).start()
    over(0, side, near_terms)

    landed(shrink.at[pl.ds(0, (n_tp - 1) * slab)], shr_recv)

    keep_b.wait()
    landed(pan_b.at[:, pl.ds(0, (n_tp - 1) * LANES)], pb_recv)

    def send_delta(k):
        peer = rep_peer(k)
        return remote(delta.at[peer], delta_in.at[rep], del_send.at[0], del_recv.at[0], (peer, t))

    for m in near_first[::-1]:
        source = lax.rem(chip + m, chips)
        place_rows, upper = packed(source)
        shrunk = shrink[place_rows, :].astype(F32)
        turned = pltpu.roll(shrunk, RANK, 1)
        in_low = jnp.where(low_lanes, jnp.where(upper, turned, shrunk), 0.0)
        in_high = jnp.where(low_lanes, 0.0, jnp.where(upper, shrunk, turned))
        mask = masks(source)
        for side_of, placed in enumerate((in_low, in_high)):
            picked = (mask * jnp.concatenate([placed] * n_tp, axis=1)).astype(BF16)
            result = nt_dot(picked, pan_b[...]).astype(BF16)
            cols = slice(side_of * half_width, (side_of + 1) * half_width)
            delta[pl.ds(2 * source, 2), :, cols] = result.reshape(2, steps * CAP, half_width)
        for f in range(2):
            if m or f:
                send_delta(2 * m + f).start()
    delta_in[rep] = delta[rep]
    over(0, side - 1, second_stage)

    last = side - 1
    base[:, :part_width] = gathered(own_y, in_y, along_y, last)
    base[:, part_width:] = gathered(own_z, in_z, along_z, last)
    landed(delta_in.at[pl.ds(0, n_rep - 1)], del_recv)
    for s in range(steps):
        rows_in = delta_in[:, s * CAP : (s + 1) * CAP, :].reshape(n_dest, width)
        base[s * rows : (s + 1) * rows, :] += ADAPTER_SCALING * dot(place[s], rows_in)
    for j in range(last):
        forward_y(j).wait_recv()
        forward_z(j).wait_recv()
    for s in range(steps):
        span = slice(s * rows, (s + 1) * rows)
        for cols, got in ((slice(0, part_width), got_a), (slice(part_width, width), got_b)):
            total = base[span, cols]
            for j in range(last):
                total = total + got[j, span, :].astype(F32)
            out[s, :, cols] = total.astype(BF16)

    for part_of in range(2):
        swap_back(part_of).wait_send()
    landed(pack_a.at[pl.ds(0, n_tp - 1)], pa_send)
    landed(pack_b.at[pl.ds(0, n_tp - 1)], pb_send)
    landed(tag_out.at[pl.ds(0, n_rep - 1)], tag_send)
    landed(disp.at[pl.ds(0, n_rep - 1)], disp_send)
    landed(part_in.at[pl.ds(1, n_tp - 1)], part_send)
    landed(shrink.at[pl.ds(0, (n_tp - 1) * slab)], shr_send)
    landed(delta.at[pl.ds(0, n_rep - 1)], del_send)
    landed(far_y, hop_y_send)
    landed(far_z, hop_z_send)
    landed(near_y, y_send)
    landed(near_z, z_send)
    landed(fwd_a, a_send)
    landed(fwd_b, b_send)


def shards(n_rep, n_tp, queries, new_kv, kv_cache, lengths, adapter_ids, owner_slot, panels, out_weight):
    side = math.isqrt(n_tp)
    steps, rows, width = queries.shape
    half = rows // 2
    heads = width // HD
    total = steps * rows
    part = width // 2
    per_request = 2 * heads * steps
    work_rows = n_rep * steps * CAP
    dma = pltpu.SemaphoreType.DMA
    vmem = pltpu.VMEM
    hop = side - 1
    scratch = [
        vmem((steps, half, width), BF16),
        vmem((steps, half, width), BF16),
        vmem((half * per_request, HD), F32),
        vmem((half * per_request, HD), F32),
        vmem((steps, half, 2 * HD), BF16),
        vmem(kv_cache.shape, BF16),
        vmem(out_weight.shape, BF16),
        vmem((n_tp, width, LANES), BF16),
        vmem((n_tp, width // 2, LANES), BF16),
        vmem((n_tp, width // 2, LANES), BF16),
        vmem((width // 2, n_tp * LANES), BF16),
        vmem((width // 2, n_tp * LANES), BF16),
        vmem((LANES, n_tp * LANES), BF16),
        vmem((steps, rows, width), BF16),
        vmem((steps, half, width), BF16),
        vmem((steps, rows, LANES), BF16),
        vmem((steps, rows, n_rep * CAP), BF16),
        vmem((2, side, total // 2, part), BF16),
        vmem((2, side, total // 2, part), BF16),
        vmem((2, side, total, part), BF16),
        vmem((2, side, total, part), BF16),
        vmem((side, total, part), F32),
        vmem((2, side, total // 2, part), BF16),
        vmem((2, side, total // 2, part), BF16),
        vmem((2, side, total, part), BF16),
        vmem((2, side, total, part), BF16),
        vmem((side, total, part), F32),
        vmem((hop, total, part), BF16),
        vmem((hop, total, part), BF16),
        vmem((hop, total, part), BF16),
        vmem((hop, total, part), BF16),
        vmem((total, width), F32),
        vmem((n_rep, steps * CAP, LANES), BF16),
        vmem((n_rep, steps * CAP, LANES), BF16),
        vmem((n_rep, steps * CAP, width), BF16),
        vmem((n_rep, steps * CAP, width), BF16),
        vmem((work_rows // 2, LANES), F32),
        vmem((n_tp, work_rows // 2 // n_tp, LANES), F32),
        vmem((work_rows // 2, LANES), BF16),
        vmem((n_rep, steps * CAP, width), BF16),
        vmem((n_rep, steps * CAP, width), BF16),
        dma((half // KV_CHUNK,)),
        dma((5,)),
        dma((n_tp,)),
        dma((2,)), dma((2,)),
        dma((1,)), dma((1,)),
        dma((1,)), dma((1,)),
        dma((2,)), dma((2,)),
        dma((1,)), dma((2, side)),
        dma((1,)), dma((2, side)),
        dma((1,)), dma((2, side)),
        dma((1,)), dma((2, side)),
        dma((1,)), dma((hop,)),
        dma((1,)), dma((hop,)),
        dma((1,)), dma((1,)),
        dma((1,)), dma((n_rep,)),
        dma((1,)), dma((1,)),
        dma((1,)), dma((1,)),
        dma((1,)), dma((1,)),
    ]
    hbm = pl.BlockSpec(memory_space=pl.ANY)
    in_vmem = pl.BlockSpec(memory_space=pltpu.VMEM)
    in_smem = pl.BlockSpec(memory_space=pltpu.SMEM)
    return pl.pallas_call(
        functools.partial(kernel, n_rep, n_tp, side),
        out_shape=jax.ShapeDtypeStruct(queries.shape, BF16),
        in_specs=[hbm, hbm, hbm, in_smem, in_vmem, in_vmem, hbm, hbm],
        out_specs=in_vmem,
        scratch_shapes=scratch,
        compiler_params=pltpu.CompilerParams(
            collective_id=0, has_side_effects=True, vmem_limit_bytes=56 * 1024 * 1024
        ),
        cost_estimate=pl.CostEstimate(
            flops=5_000_000_000, bytes_accessed=20_000_000, transcendentals=600_000
        ),
    )(queries, new_kv, kv_cache, lengths, adapter_ids, owner_slot.reshape(1, -1), panels, out_weight)


def solution(mesh):
    placed = (
        P(None, "rep", "tp"),
        P(None, "rep", None),
        P("rep", None, "tp"),
        P(None, "rep"),
        P(None, "rep"),
        P(),
        P(("rep", "tp"), None, None),
        P("tp", None),
    )
    return jax.shard_map(
        functools.partial(shards, mesh.shape["rep"], mesh.shape["tp"]),
        mesh=mesh, in_specs=placed, out_specs=P(None, "rep", "tp"), check_vma=False,
    )
```
